256 devices in a mesh: ctx: 32 (over z, y_lo, core), chan: 8 (over y_hi, x).
Axes of the slice: x: 4, y: 4 (y_hi: 2, y_lo: 2; y = y_hi * 2 + y_lo), z: 8, core: 2. Of those that a mesh axis runs over, the one named last changes fastest.
Arguments:
- sequence: float32 [32, 524288], P('chan', 'ctx'), may hold values from -6 to 6
- filter_taps: float32 [2, 524288], P(None, 'ctx'), may hold values from -6 to 6
- skip_gain: float32 [32], P('chan'), may hold values from 0.5 to 1.5
- cotangent: float32 [32, 524288], P('chan', 'ctx'), may hold values from -6 to 6
Outputs:
- convolved: float32 [32, 524288], P('chan', 'ctx')
- seq_grad: float32 [32, 524288], P('chan', 'ctx')
- filter_grad: float32 [2, 524288], P(None, 'ctx')
The draws below stay inside these ranges and needn't reach their ends.
All inputs are finite; a program needn't handle non-finite values.
Results may differ from the reference program's by a relative error of at most 0.0003.
Values sent between devices are 32-bit elements; how exact they have to be, the bound alone decides.
No kernel may reach another device: no remote copies, remote signals or barrier semaphores. Data moves between devices by JAX's collectives and lax.ppermute only.
A program may use at most 128 MiB of HBM per device.

```python
import jax
import jax.numpy as jnp
from jax import lax

CH = 32
FG = 2
LEN = 524288


def levels(rng, shape, cuts, smallest, top_value):
    factor_of = 1.0
    for position, shards_of in cuts:
        steps = jax.random.uniform(jax.random.fold_in(jax.random.fold_in(rng, 6), position), (shards_of,), jnp.float32, smallest / len(cuts), top_value / len(cuts))
        factor_of = factor_of * jnp.repeat(jnp.exp(steps), shape[position] // shards_of).reshape((-1,) + (1,) * (len(shape) - 1 - position))
    return factor_of


def scatter_about(rng, shape, width, reach, pieces=(), held_as=jnp.bfloat16):
    loudness = levels(rng, shape, pieces, -0.22, 0.18) if pieces else 1.0
    values = jax.random.normal(rng, shape, jnp.float32) * width * loudness
    return jnp.minimum(jnp.maximum(values, -reach), reach).astype(held_as)


def setup_inputs(seed: int = 0) -> dict:
    seeds = jax.random.split(jax.random.key(seed), 5)
    return {
        "sequence": scatter_about(seeds[0], (CH, LEN), 1.0, 6.0, ((0, 8), (1, 32)), jnp.float32),
        "filter_taps": scatter_about(seeds[1], (FG, LEN), 1.0, 6.0, ((1, 32),), jnp.float32),
        "skip_gain": jnp.clip(0.5 + 1.0 * jax.random.uniform(seeds[2], (CH,), jnp.float32) ** levels(seeds[2], (CH,), ((0, 8),), -0.2, 0.2), 0.5, 1.5),
        "cotangent": scatter_about(seeds[3], (CH, LEN), 1.0, 6.0, ((0, 8), (1, 32)), jnp.float32),
    }


def reference(sequence, filter_taps, skip_gain, cotangent):
    length = sequence.shape[1]
    padded_points = 2 * length
    norm_scale = length ** -0.5
    filter_spectra = jnp.fft.rfft(filter_taps, n=padded_points, axis=1)

    def channel_terms(channel):
        signal = sequence[channel]
        grad_row = cotangent[channel]
        spectrum = filter_spectra[(channel // 2) % FG]
        signal_spec = jnp.fft.rfft(signal, n=padded_points)
        grad_spec = jnp.fft.rfft(grad_row, n=padded_points)
        convolution = jnp.fft.irfft(spectrum * signal_spec, n=padded_points)[:length] * norm_scale
        grad_terms = jnp.fft.irfft(jnp.conj(spectrum) * grad_spec, n=padded_points)[:length] * norm_scale
        tap_terms = jnp.fft.irfft(jnp.conj(signal_spec) * grad_spec, n=padded_points)[:length] * norm_scale
        skip_value = skip_gain[channel]
        return convolution + skip_value * signal, grad_terms + skip_value * grad_row, tap_terms

    convolved, seq_grad, per_channel = lax.map(channel_terms, jnp.arange(CH, dtype=jnp.int32))
    filter_grad = per_channel.reshape(CH // (2 * FG), FG, 2, length).sum(axis=(0, 2))
    return convolved, seq_grad, filter_grad
```

```python
import numpy as np
import jax
import jax.numpy as jnp
from jax import lax
from jax.experimental import pallas as pl
from jax.experimental.pallas import tpu as pltpu
from jax.sharding import PartitionSpec as P
import ml_dtypes

SIDE = 128
BLOCK = SIDE * SIDE
BLOCKS = 32
SUB = SIDE // BLOCKS
ROWS = 2 * SIDE
PAD = 4
TILE = 4
VMEM_LIMIT = 40 * 1024 * 1024


def two_parts(table):
    high = table.astype(ml_dtypes.bfloat16)
    low = (table - high.astype(np.float64)).astype(ml_dtypes.bfloat16)
    return high, low


def make_tables():
    row = np.arange(ROWS)
    coarse = SUB * (row // (2 * SUB)) + row % SUB
    signal = (row // SUB) % 2
    position = np.arange(SIDE)
    turn = 2.0 * np.pi
    angle = turn * ((coarse[:, None] + 0.25) * position[None, :] / SIDE)
    own = (signal[:, None] == np.arange(2)[None, :])[:, :, None]
    cosine = (own * np.cos(angle)[:, None, :]).reshape(ROWS, 2 * SIDE)
    sine = (own * np.sin(angle)[:, None, :]).reshape(ROWS, 2 * SIDE)
    forward_outer = np.concatenate([cosine, -sine], axis=0)
    factor = (BLOCKS * BLOCK) ** (-0.5) / BLOCK
    inverse_outer = factor * np.concatenate([cosine.T, -sine.T], axis=1)
    angle = turn * ((coarse[:, None] + 0.25) * position[None, :] / BLOCK)
    twist = np.stack([np.cos(angle), np.sin(angle)]).astype(np.float32)
    angle = turn * ((position[:, None] * position[None, :]) % SIDE / SIDE)
    cosine, sine = np.cos(angle), np.sin(angle)
    forward_inner = np.block([[cosine, -sine], [sine, cosine]])
    inverse_inner = np.block([[cosine, sine], [-sine, cosine]])
    return (
        two_parts(forward_outer) + two_parts(forward_inner),
        two_parts(inverse_inner) + two_parts(inverse_outer),
        twist,
    )


FORWARD_TABLES, INVERSE_TABLES, TWIST = make_tables()


def split(values):
    high = values.astype(jnp.bfloat16)
    return high, (values - high.astype(jnp.float32)).astype(jnp.bfloat16)


def dot(left, right):
    return jnp.dot(left, right, preferred_element_type=jnp.float32)


def dot_three(left, right):
    return dot(left[0], right[0]) + (dot(left[0], right[1]) + dot(left[1], right[0]))


def spread(source, rows, count):
    for a in range(SIDE):
        rows[pl.ds(a, count, stride=SIDE), :] = source[:, a * SIDE : (a + 1) * SIDE]


def forward_kernel(seq_ref, cot_ref, taps_ref, oh_ref, ol_ref, ih_ref, il_ref, twist_ref, out_ref, rows):
    spread(seq_ref, rows.at[0 : 4 * SIDE], 4)
    spread(cot_ref, rows.at[4 * SIDE : 8 * SIDE], 4)
    spread(taps_ref, rows.at[8 * SIDE : 10 * SIDE], 2)

    def row(index):
        return rows[index * SIDE : (index + 1) * SIDE, :]

    firsts = (0, 1, 4, 5, 8)
    seconds = (2, 3, 6, 7, 9)
    signals = jnp.concatenate(
        [
            jnp.concatenate([row(i) for i in firsts], axis=1),
            jnp.concatenate([row(i) for i in seconds], axis=1),
        ],
        axis=0,
    )
    opened = dot_three((oh_ref[...], ol_ref[...]), split(signals))
    cosine, sine = twist_ref[0], twist_ref[1]
    inner = (ih_ref[...], il_ref[...])
    for p in range(5):
        real = opened[:ROWS, p * SIDE : (p + 1) * SIDE]
        imag = opened[ROWS:, p * SIDE : (p + 1) * SIDE]
        both = jnp.concatenate([real * cosine + imag * sine, imag * cosine - real * sine], axis=1)
        spectrum = dot_three(split(both), inner)
        out_ref[:, 16 * p : 16 * p + 8, :] = spectrum[:, :SIDE].reshape(BLOCKS, 8, SIDE)
        out_ref[:, 16 * p + 8 : 16 * p + 16, :] = spectrum[:, SIDE:].reshape(BLOCKS, 8, SIDE)


def forward_blocks(sequence, cotangent, taps):
    tables = [jnp.asarray(t) for t in FORWARD_TABLES]
    return pl.pallas_call(
        forward_kernel,
        out_shape=jax.ShapeDtypeStruct((BLOCKS, 80, SIDE), jnp.float32),
        in_specs=[pl.BlockSpec(memory_space=pltpu.VMEM)] * 8,
        out_specs=pl.BlockSpec(memory_space=pltpu.VMEM),
        scratch_shapes=[pltpu.VMEM((10 * SIDE, SIDE), jnp.float32)],
        compiler_params=pltpu.CompilerParams(vmem_limit_bytes=VMEM_LIMIT),
        name="forward_blocks",
    )(sequence, cotangent, taps, *tables, jnp.asarray(TWIST))


def middle_kernel(in_ref, out_ref, kernels):
    for slot, p in enumerate((4, 0, 1)):
        kernels[slot, :PAD] = jnp.zeros((PAD, 16, SIDE), jnp.float32)
        top = 16 * p
        kernels[slot, PAD, :, :] = in_ref[0, top : top + 16, :]

        def fill(j, carry, slot=slot, top=top):
            kernels[slot, PAD + j, 0:8, :] = in_ref[j, top : top + 8, :] - in_ref[j - 1, top + 8 : top + 16, :]
            kernels[slot, PAD + j, 8:16, :] = in_ref[j, top + 8 : top + 16, :] + in_ref[j - 1, top : top + 8, :]
            return carry

        lax.fori_loop(1, BLOCKS, fill, 0, unroll=4)

    tiles = BLOCKS // TILE

    def products(slot, p, lag0, b0, causal, totals):
        window = [
            (kernels[slot, PAD + lag0 + d, 0:8, :], kernels[slot, PAD + lag0 + d, 8:16, :])
            for d in range(1 - TILE, TILE)
        ]
        totals = list(totals)
        for s in range(TILE):
            xr = in_ref[b0 + s, 16 * p : 16 * p + 8, :]
            xi = in_ref[b0 + s, 16 * p + 8 : 16 * p + 16, :]
            for i in range(TILE):
                kr, ki = window[TILE - 1 + ((i - s) if causal else (s - i))]
                tr, ti = totals[2 * i], totals[2 * i + 1]
                if causal:
                    totals[2 * i] = tr + kr * xr - ki * xi
                    totals[2 * i + 1] = ti + kr * xi + ki * xr
                else:
                    totals[2 * i] = tr + kr * xr + ki * xi
                    totals[2 * i + 1] = ti + kr * xi - ki * xr
        return tuple(totals)

    def store(m0, p, totals):
        for i in range(TILE):
            out_ref[m0 + i, 16 * p : 16 * p + 8, :] = totals[2 * i]
            out_ref[m0 + i, 16 * p + 8 : 16 * p + 16, :] = totals[2 * i + 1]

    zero = tuple(jnp.zeros((8, SIDE), jnp.float32) for _ in range(2 * TILE))

    def one_tile(t, carry):
        m0 = t * TILE
        for p in (0, 1):
            totals = lax.fori_loop(
                0, t + 1, lambda u, c, p=p: products(0, p, (t - u) * TILE, u * TILE, True, c), zero
            )
            store(m0, p, totals)
        for p in (2, 3):
            totals = lax.fori_loop(
                t, tiles, lambda u, c, p=p: products(0, p, (u - t) * TILE, u * TILE, False, c), zero
            )
            store(m0, p, totals)
        totals = zero
        for q in (0, 1):
            totals = lax.fori_loop(
                t, tiles, lambda u, c, q=q: products(1 + q, 2 + q, (u - t) * TILE, u * TILE, False, c), totals
            )
        store(m0, 4, totals)
        return carry

    lax.fori_loop(0, tiles, one_tile, 0)


def middle_blocks(spectra):
    return pl.pallas_call(
        middle_kernel,
        out_shape=jax.ShapeDtypeStruct((BLOCKS, 80, SIDE), jnp.float32),
        in_specs=[pl.BlockSpec(memory_space=pltpu.VMEM)],
        out_specs=pl.BlockSpec(memory_space=pltpu.VMEM),
        scratch_shapes=[pltpu.VMEM((3, PAD + BLOCKS, 16, SIDE), jnp.float32)],
        compiler_params=pltpu.CompilerParams(vmem_limit_bytes=VMEM_LIMIT),
        name="middle_blocks",
    )(spectra)


def inverse_kernel(
    in_ref, seq_ref, cot_ref, skip_ref, ih_ref, il_ref, oh_ref, ol_ref, twist_ref, y_ref, g_ref, f_ref, rows
):
    cosine, sine = twist_ref[0], twist_ref[1]
    inner = (ih_ref[...], il_ref[...])
    closing = []
    for p in range(5):
        both = jnp.concatenate(
            [
                in_ref[:, 16 * p : 16 * p + 8, :].reshape(ROWS, SIDE),
                in_ref[:, 16 * p + 8 : 16 * p + 16, :].reshape(ROWS, SIDE),
            ],
            axis=1,
        )
        turned = dot_three(split(both), inner)
        real, imag = turned[:, :SIDE], turned[:, SIDE:]
        closing.append(jnp.concatenate([real * cosine - imag * sine, imag * cosine + real * sine], axis=0))
    closed = dot_three((oh_ref[...], ol_ref[...]), split(jnp.concatenate(closing, axis=1)))
    firsts = (0, 1, 4, 5, 8)
    seconds = (2, 3, 6, 7, 9)
    for p in range(5):
        for half, place in enumerate((firsts[p], seconds[p])):
            rows[place * SIDE : (place + 1) * SIDE, :] = closed[
                half * SIDE : (half + 1) * SIDE, p * SIDE : (p + 1) * SIDE
            ]
    skip = jnp.broadcast_to(skip_ref[...], (4, SIDE))
    for a in range(SIDE):
        lanes = slice(a * SIDE, (a + 1) * SIDE)
        y_ref[:, lanes] = rows[pl.ds(a, 4, stride=SIDE), :] + skip * seq_ref[:, lanes]
        g_ref[:, lanes] = rows[pl.ds(4 * SIDE + a, 4, stride=SIDE), :] + skip * cot_ref[:, lanes]
        f_ref[:, lanes] = rows[pl.ds(8 * SIDE + a, 2, stride=SIDE), :]


def inverse_blocks(products, sequence, cotangent, skip_gain):
    tables = [jnp.asarray(t) for t in INVERSE_TABLES]
    return pl.pallas_call(
        inverse_kernel,
        out_shape=(
            jax.ShapeDtypeStruct((4, BLOCK), jnp.float32),
            jax.ShapeDtypeStruct((4, BLOCK), jnp.float32),
            jax.ShapeDtypeStruct((2, BLOCK), jnp.float32),
        ),
        in_specs=[pl.BlockSpec(memory_space=pltpu.VMEM)] * 9,
        out_specs=(pl.BlockSpec(memory_space=pltpu.VMEM),) * 3,
        scratch_shapes=[pltpu.VMEM((10 * SIDE, SIDE), jnp.float32)],
        compiler_params=pltpu.CompilerParams(vmem_limit_bytes=VMEM_LIMIT),
        name="inverse_blocks",
    )(products, sequence, cotangent, skip_gain[:, None], *tables, jnp.asarray(TWIST))


def exchange(blocks):
    return lax.all_to_all(blocks, "ctx", split_axis=0, concat_axis=0, tiled=True)


def sum_over_chan(values, size):
    for flip in (1, 3, 4):
        if flip < size:
            values = values + lax.ppermute(values, "chan", [(i, i ^ flip) for i in range(size)])
    return values


def solution(mesh):
    chan = mesh.shape["chan"]

    def body(sequence, filter_taps, skip_gain, cotangent):
        spectra = exchange(forward_blocks(sequence, cotangent, filter_taps))
        products = exchange(middle_blocks(spectra))
        convolved, seq_grad, taps_grad = inverse_blocks(products, sequence, cotangent, skip_gain)
        return convolved, seq_grad, sum_over_chan(taps_grad, chan)

    return jax.shard_map(
        body,
        mesh=mesh,
        in_specs=(P("chan", "ctx"), P(None, "ctx"), P("chan"), P("chan", "ctx")),
        out_specs=(P("chan", "ctx"), P("chan", "ctx"), P(None, "ctx")),
        check_vma=False,
    )
```

```python
import numpy as np
import jax
import jax.numpy as jnp
from jax import lax
from jax.experimental import pallas as pl
from jax.experimental.pallas import tpu as pltpu
from jax.sharding import PartitionSpec as P

SIDE = 128
BLOCK = SIDE * SIDE
BLOCKS = 32
SUB = SIDE // BLOCKS
ROWS = 2 * SIDE
POINTS = 2 * BLOCKS
VMEM_LIMIT = 40 * 1024 * 1024


def make_tables():
    row = np.arange(ROWS)
    coarse = SUB * (row // (2 * SUB)) + row % SUB
    signal = (row // SUB) % 2
    position = np.arange(SIDE)
    turn = 2.0 * np.pi
    angle = turn * ((coarse[:, None] + 0.25) * position[None, :] / SIDE)
    own = (signal[:, None] == np.arange(2)[None, :])[:, :, None]
    cosine = (own * np.cos(angle)[:, None, :]).reshape(ROWS, 2 * SIDE)
    sine = (own * np.sin(angle)[:, None, :]).reshape(ROWS, 2 * SIDE)
    forward_outer = np.concatenate([cosine, -sine], axis=0)
    factor = (BLOCKS * BLOCK) ** (-0.5) / BLOCK
    inverse_outer = factor * np.concatenate([cosine.T, -sine.T], axis=1)
    angle = turn * ((coarse[:, None] + 0.25) * position[None, :] / BLOCK)
    twist = np.stack([np.cos(angle), np.sin(angle)]).astype(np.float32)
    angle = turn * ((position[:, None] * position[None, :]) % SIDE / SIDE)
    cosine, sine = np.cos(angle), np.sin(angle)
    forward_inner = np.block([[cosine, -sine], [sine, cosine]])
    inverse_inner = np.block([[cosine, sine], [-sine, cosine]])
    single = np.float32
    return (
        (forward_outer.astype(single), forward_inner.astype(single), twist),
        (inverse_inner.astype(single), inverse_outer.astype(single), twist),
    )


def make_block_tables():
    block = np.arange(BLOCKS)
    point = np.arange(POINTS)
    angle = 2.0 * np.pi * ((point[:, None] * block[None, :]) % POINTS) / POINTS
    cosine, sine = np.cos(angle), np.sin(angle)
    tables = [np.block([[cosine, sine], [-sine, cosine]]).astype(np.float32)]
    step = np.exp(-2j * np.pi * point / POINTS)
    for spill in (1.0 + 1j * step, 1.0 - 1j * np.conj(step)):
        back = np.exp(1j * angle.T) * spill[None, :] / POINTS
        tables.append(np.block([[back.real, -back.imag], [back.imag, back.real]]).astype(np.float32))
    return tables


FORWARD_TABLES, INVERSE_TABLES = make_tables()
BLOCK_TABLES = make_block_tables()


def split(values):
    high = values.astype(jnp.bfloat16)
    return high, (values - high.astype(jnp.float32)).astype(jnp.bfloat16)


def dot(left, right):
    return jnp.dot(left, right, preferred_element_type=jnp.float32)


def dot_three(left, right):
    return dot(left[0], right[0]) + (dot(left[0], right[1]) + dot(left[1], right[0]))


def spread(source, rows, count):
    for a in range(SIDE):
        rows[pl.ds(a, count, stride=SIDE), :] = source[:, a * SIDE : (a + 1) * SIDE]


def forward_kernel(*refs):
    sources, out_ref, held, rows, sems = refs[:6], refs[6], refs[7:13], refs[13], refs[14]
    copies = [pltpu.make_async_copy(s, h, sems.at[i]) for i, (s, h) in enumerate(zip(sources, held))]
    for copy in copies:
        copy.start()
    seq_ref, cot_ref, taps_ref, outer_ref, inner_ref, twist_ref = held
    copies[0].wait()
    spread(seq_ref, rows.at[0 : 4 * SIDE], 4)
    copies[1].wait()
    spread(cot_ref, rows.at[4 * SIDE : 8 * SIDE], 4)
    copies[2].wait()
    spread(taps_ref, rows.at[8 * SIDE : 10 * SIDE], 2)
    for copy in copies[3:]:
        copy.wait()

    def row(index):
        return rows[index * SIDE : (index + 1) * SIDE, :]

    signals = jnp.concatenate(
        [
            jnp.concatenate([row(i) for i in (0, 1, 4, 5, 8)], axis=1),
            jnp.concatenate([row(i) for i in (2, 3, 6, 7, 9)], axis=1),
        ],
        axis=0,
    )
    opened = dot_three(split(outer_ref[...]), split(signals))
    cosine, sine = twist_ref[0], twist_ref[1]
    inner = split(inner_ref[...])
    for p in range(5):
        real = opened[:ROWS, p * SIDE : (p + 1) * SIDE]
        imag = opened[ROWS:, p * SIDE : (p + 1) * SIDE]
        both = jnp.concatenate([real * cosine + imag * sine, imag * cosine - real * sine], axis=1)
        spectrum = dot_three(split(both), inner)
        out_ref[:, 16 * p : 16 * p + 8, :] = spectrum[:, :SIDE].reshape(BLOCKS, 8, SIDE)
        out_ref[:, 16 * p + 8 : 16 * p + 16, :] = spectrum[:, SIDE:].reshape(BLOCKS, 8, SIDE)


def forward_blocks(sequence, cotangent, taps):
    operands = (sequence, cotangent, taps) + tuple(jnp.asarray(t) for t in FORWARD_TABLES)
    return pl.pallas_call(
        forward_kernel,
        out_shape=jax.ShapeDtypeStruct((BLOCKS, 80, SIDE), jnp.float32),
        in_specs=[pl.BlockSpec(memory_space=pl.ANY)] * 6,
        out_specs=pl.BlockSpec(memory_space=pltpu.VMEM),
        scratch_shapes=[pltpu.VMEM(v.shape, v.dtype) for v in operands]
        + [pltpu.VMEM((10 * SIDE, SIDE), jnp.float32), pltpu.SemaphoreType.DMA((6,))],
        compiler_params=pltpu.CompilerParams(vmem_limit_bytes=60 * 1024 * 1024),
        name="forward_blocks",
    )(*operands)


def middle_kernel(in_ref, there_ref, back_ref, adjoint_ref, out_ref, taps_ref):
    def three(values):
        high, low = split(values)
        return jnp.concatenate([high, low, high], axis=0)

    def wide(table):
        high, low = split(table[...])
        return jnp.concatenate([high, high, low], axis=1)

    there, back, adjoint = wide(there_ref), wide(back_ref), wide(adjoint_ref)

    def pair(p):
        halves = [
            jnp.concatenate(
                [in_ref[pl.ds(16 * p + 8 * h + r, BLOCKS, stride=80), :] for r in range(8)], axis=1
            )
            for h in range(2)
        ]
        points = dot(there, three(jnp.concatenate(halves, axis=0)))
        return points[:POINTS], points[POINTS:]

    def store(ref, p, width, table, real, imag):
        blocks = dot(table, three(jnp.concatenate([real, imag], axis=0)))
        for h in range(2):
            for r in range(8):
                ref[pl.ds(16 * p + 8 * h + r, BLOCKS, stride=width), :] = blocks[
                    BLOCKS * h : BLOCKS * (h + 1), r * SIDE : (r + 1) * SIDE
                ]

    signals = [pair(p) for p in range(4)]
    tap_real = tap_imag = 0.0
    for q in range(2):
        (xr, xi), (gr, gi) = signals[q], signals[2 + q]
        tap_real = tap_real + (xr * gr + xi * gi)
        tap_imag = tap_imag + (xr * gi - xi * gr)
    store(taps_ref, 0, 16, adjoint, tap_real, tap_imag)
    hr, hi = pair(4)
    for q in range(2):
        (xr, xi), (gr, gi) = signals[q], signals[2 + q]
        store(out_ref, q, 64, back, hr * xr - hi * xi, hr * xi + hi * xr)
        store(out_ref, 2 + q, 64, adjoint, hr * gr + hi * gi, hr * gi - hi * gr)


def middle_blocks(spectra):
    tables = [jnp.asarray(t) for t in BLOCK_TABLES]
    products, taps = pl.pallas_call(
        middle_kernel,
        out_shape=(
            jax.ShapeDtypeStruct((BLOCKS * 64, SIDE), jnp.float32),
            jax.ShapeDtypeStruct((BLOCKS * 16, SIDE), jnp.float32),
        ),
        in_specs=[pl.BlockSpec(memory_space=pltpu.VMEM)] * 4,
        out_specs=(pl.BlockSpec(memory_space=pltpu.VMEM),) * 2,
        compiler_params=pltpu.CompilerParams(vmem_limit_bytes=VMEM_LIMIT),
        name="middle_blocks",
    )(spectra.reshape(BLOCKS * 80, SIDE), *tables)
    return products.reshape(BLOCKS, 64, SIDE), taps.reshape(BLOCKS, 16, SIDE)


def closed_blocks(in_ref, inner_ref, outer_ref, twist_ref, rows, count):
    cosine, sine = twist_ref[0], twist_ref[1]
    inner = split(inner_ref[...])
    closing = []
    for p in range(count):
        both = jnp.concatenate(
            [
                in_ref[:, 16 * p : 16 * p + 8, :].reshape(ROWS, SIDE),
                in_ref[:, 16 * p + 8 : 16 * p + 16, :].reshape(ROWS, SIDE),
            ],
            axis=1,
        )
        turned = dot_three(split(both), inner)
        real, imag = turned[:, :SIDE], turned[:, SIDE:]
        closing.append(jnp.concatenate([real * cosine - imag * sine, imag * cosine + real * sine], axis=0))
    closed = dot_three(split(outer_ref[...]), split(jnp.concatenate(closing, axis=1)))
    for p in range(count):
        for half in range(2):
            place = 4 * (p // 2) + 2 * half + p % 2 if count > 1 else half
            rows[place * SIDE : (place + 1) * SIDE, :] = closed[
                half * SIDE : (half + 1) * SIDE, p * SIDE : (p + 1) * SIDE
            ]


def taps_kernel(in_ref, inner_ref, outer_ref, twist_ref, f_ref, rows):
    closed_blocks(in_ref, inner_ref, outer_ref, twist_ref, rows, 1)
    for a in range(SIDE):
        f_ref[:, a * SIDE : (a + 1) * SIDE] = rows[pl.ds(a, 2, stride=SIDE), :]


def inverse_kernel(
    in_ref, seq_ref, cot_ref, skip_ref, inner_ref, outer_ref, twist_ref, y_ref, g_ref, rows
):
    closed_blocks(in_ref, inner_ref, outer_ref, twist_ref, rows, 4)
    skip = jnp.broadcast_to(skip_ref[...], (4, SIDE))
    for a in range(SIDE):
        lanes = slice(a * SIDE, (a + 1) * SIDE)
        y_ref[:, lanes] = rows[pl.ds(a, 4, stride=SIDE), :] + skip * seq_ref[:, lanes]
        g_ref[:, lanes] = rows[pl.ds(4 * SIDE + a, 4, stride=SIDE), :] + skip * cot_ref[:, lanes]


def taps_blocks(products):
    tables = [jnp.asarray(t) for t in INVERSE_TABLES]
    return pl.pallas_call(
        taps_kernel,
        out_shape=jax.ShapeDtypeStruct((2, BLOCK), jnp.float32),
        in_specs=[pl.BlockSpec(memory_space=pltpu.VMEM)] * 4,
        out_specs=pl.BlockSpec(memory_space=pltpu.VMEM),
        scratch_shapes=[pltpu.VMEM((2 * SIDE, SIDE), jnp.float32)],
        compiler_params=pltpu.CompilerParams(vmem_limit_bytes=VMEM_LIMIT),
        name="taps_blocks",
    )(products, *tables)


def inverse_blocks(products, sequence, cotangent, skip_gain):
    tables = [jnp.asarray(t) for t in INVERSE_TABLES]
    return pl.pallas_call(
        inverse_kernel,
        out_shape=(jax.ShapeDtypeStruct((4, BLOCK), jnp.float32),) * 2,
        in_specs=[pl.BlockSpec(memory_space=pltpu.VMEM)] * 7,
        out_specs=(pl.BlockSpec(memory_space=pltpu.VMEM),) * 2,
        scratch_shapes=[pltpu.VMEM((8 * SIDE, SIDE), jnp.float32)],
        compiler_params=pltpu.CompilerParams(vmem_limit_bytes=VMEM_LIMIT),
        name="inverse_blocks",
    )(products, sequence, cotangent, skip_gain[:, None], *tables)


def exchange(blocks):
    return lax.all_to_all(blocks, "ctx", split_axis=0, concat_axis=0, tiled=True)


def sum_over_chan(values, size):
    for flip in (1, 3, 4):
        if flip < size:
            values = values + lax.ppermute(values, "chan", [(i, i ^ flip) for i in range(size)])
    return values


def solution(mesh):
    chan = mesh.shape["chan"]

    def body(sequence, filter_taps, skip_gain, cotangent):
        spectra = exchange(forward_blocks(sequence, cotangent, filter_taps))
        products, taps = middle_blocks(spectra)
        taps = exchange(taps)
        taps, products = lax.optimization_barrier((taps, products))
        taps_grad = sum_over_chan(taps_blocks(taps), chan)
        convolved, seq_grad = inverse_blocks(exchange(products), sequence, cotangent, skip_gain)
        return convolved, seq_grad, taps_grad

    return jax.shard_map(
        body,
        mesh=mesh,
        in_specs=(P("chan", "ctx"), P(None, "ctx"), P("chan"), P("chan", "ctx")),
        out_specs=(P("chan", "ctx"), P("chan", "ctx"), P(None, "ctx")),
        check_vma=False,
    )
```

```python
import numpy as np
import jax
import jax.numpy as jnp
from jax import lax
from jax.experimental import pallas as pl
from jax.experimental.pallas import tpu as pltpu
from jax.sharding import PartitionSpec as P

SIDE = 128
BLOCK = SIDE * SIDE
BLOCKS = 32
SUB = SIDE // BLOCKS
POINTS = 2 * BLOCKS
CHAN = 8
OUT_ROWS = 66
BACK_ROWS = 64
TAPS_ROWS = 16
PAIRS = ((0, 2), (1, 3), (4, 6), (5, 7), (8, 9))
VMEM_LIMIT = 40 * 1024 * 1024
VMEM_FULL = 60 * 1024 * 1024


def make_tables():
    digit = np.arange(SIDE)
    turn = 2.0 * np.pi
    single = np.float32
    angle = turn * ((digit[:, None] + 0.25) * digit[None, :] / SIDE)
    cosine, sine = np.cos(angle), np.sin(angle)
    forward_outer = np.concatenate([cosine, -sine], axis=0)
    factor = (BLOCKS * BLOCK) ** (-0.5) / BLOCK
    inverse_outer = factor * np.concatenate([cosine.T, -sine.T], axis=1)
    angle = turn * ((digit[:, None] + 0.25) * digit[None, :] / BLOCK)
    twist = np.stack([np.cos(angle), np.sin(angle)])
    angle = turn * ((digit[:, None] * digit[None, :]) % SIDE / SIDE)
    cosine, sine = np.cos(angle), np.sin(angle)
    forward_inner = np.block([[cosine, -sine], [sine, cosine]])
    inverse_inner = np.block([[cosine, sine], [-sine, cosine]])
    return (
        tuple(t.astype(single) for t in (forward_outer, forward_inner, twist)),
        tuple(t.astype(single) for t in (inverse_inner, inverse_outer, twist)),
    )


def make_block_tables():
    block = np.arange(BLOCKS)
    point = np.arange(POINTS)
    angle = 2.0 * np.pi * ((point[:, None] * block[None, :]) % POINTS) / POINTS
    cosine, sine = np.cos(angle), np.sin(angle)
    tables = [np.block([[cosine, sine], [-sine, cosine]])]
    step = np.exp(-2j * np.pi * point / POINTS)
    for spill in (1.0 + 1j * step, 1.0 - 1j * np.conj(step)):
        back = np.exp(1j * angle.T) * spill[None, :] / POINTS
        tables.append(np.block([[back.real, -back.imag], [back.imag, back.real]]))
    return tuple(t.astype(np.float32) for t in tables)


FORWARD_TABLES, INVERSE_TABLES = make_tables()
THERE, BACK, ADJOINT = make_block_tables()


def split(values):
    high = values.astype(jnp.bfloat16)
    return high, (values - high.astype(jnp.float32)).astype(jnp.bfloat16)


def dot(left, right):
    return jnp.dot(left, right, preferred_element_type=jnp.float32)


def dot_three(left, right):
    (lh, ll), (rh, rl) = split(left), split(right)
    return dot(lh, rh) + (dot(lh, rl) + dot(ll, rh))


def dot_wide(left, right):
    (lh, ll), (rh, rl) = split(left), split(right)
    return dot(jnp.concatenate([lh, lh, ll], axis=1), jnp.concatenate([rh, rl, rh], axis=0))


def call(kernel, name, out_shape, operands, scratch=(), own_copies=False):
    space = pl.ANY if own_copies else pltpu.VMEM
    many = isinstance(out_shape[0], tuple)
    shapes = tuple(jax.ShapeDtypeStruct(s, jnp.float32) for s in (out_shape if many else (out_shape,)))
    outs = (pl.BlockSpec(memory_space=pltpu.VMEM),) * len(shapes)
    return pl.pallas_call(
        kernel,
        out_shape=shapes if many else shapes[0],
        in_specs=[pl.BlockSpec(memory_space=space)] * len(operands),
        out_specs=outs if many else outs[0],
        scratch_shapes=list(scratch),
        compiler_params=pltpu.CompilerParams(vmem_limit_bytes=VMEM_FULL if own_copies else VMEM_LIMIT),
        name=name,
    )(*operands)


def spread(source, rows, first, count):
    for a in range(SIDE):
        rows[pl.ds(first * SIDE + a, count, stride=SIDE), :] = source[:, a * SIDE : (a + 1) * SIDE]


def forward_kernel(*refs):
    sources, out_ref, held, rows, spectra, sems = refs[:6], refs[6], refs[7:13], refs[13], refs[14], refs[15]
    copies = [pltpu.make_async_copy(s, h, sems.at[i]) for i, (s, h) in enumerate(zip(sources, held))]
    for copy in copies:
        copy.start()
    seq_ref, cot_ref, taps_ref, outer_ref, inner_ref, twist_ref = held
    copies[0].wait()
    spread(seq_ref, rows, 0, 4)
    copies[1].wait()
    spread(cot_ref, rows, 4, 4)
    copies[2].wait()
    spread(taps_ref, rows, 8, 2)
    for copy in copies[3:]:
        copy.wait()

    signals = jnp.concatenate([rows[i * SIDE : (i + 1) * SIDE, :] for i in range(10)], axis=1)
    opened = dot_wide(outer_ref[...], signals)
    cosine, sine = twist_ref[0], twist_ref[1]
    inner = inner_ref[...]
    chan = lax.axis_index("chan")
    for p, pair in enumerate(PAIRS):
        twisted = []
        for i in pair:
            real = opened[:SIDE, i * SIDE : (i + 1) * SIDE]
            imag = opened[SIDE:, i * SIDE : (i + 1) * SIDE]
            twisted.append(jnp.concatenate([real * cosine + imag * sine, imag * cosine - real * sine], axis=1))
        spectrum = dot_three(jnp.concatenate(twisted, axis=0), inner)
        for h in range(2):
            held_rows = spectra.at[2 * p + h]
            held_rows[...] = spectrum[:, h * SIDE : (h + 1) * SIDE]
            picked = [held_rows[pl.ds((r // SUB) * SIDE + r % SUB, BLOCKS, stride=SUB), :] for r in range(8)]
            if p < 4:
                for r in range(8):
                    out_ref[pl.ds(16 * p + 8 * h + r, BLOCKS, stride=OUT_ROWS), :] = picked[r]
            else:
                share = picked[0]
                for r in range(1, 8):
                    share = jnp.where(chan == r, picked[r], share)
                out_ref[pl.ds(64 + h, BLOCKS, stride=OUT_ROWS), :] = share


def forward_blocks(sequence, cotangent, taps):
    operands = (sequence, cotangent, taps) + tuple(jnp.asarray(t) for t in FORWARD_TABLES)
    scratch = [pltpu.VMEM(v.shape, v.dtype) for v in operands] + [
        pltpu.VMEM((10 * SIDE, SIDE), jnp.float32),
        pltpu.VMEM((10, 2 * SIDE, SIDE), jnp.float32),
        pltpu.SemaphoreType.DMA((6,)),
    ]
    return call(forward_kernel, "forward_blocks", (BLOCKS * OUT_ROWS, SIDE), operands, scratch, True)


def points_of(in_ref, there, p):
    halves = [
        jnp.concatenate(
            [in_ref[pl.ds(16 * p + 8 * h + r, BLOCKS, stride=OUT_ROWS), :] for r in range(8)], axis=1
        )
        for h in range(2)
    ]
    points = dot_wide(there, jnp.concatenate(halves, axis=0))
    return points[:POINTS], points[POINTS:]


def blocks_of(ref, p, width, table, real, imag):
    blocks = dot_wide(table, jnp.concatenate([real, imag], axis=0))
    for h in range(2):
        for r in range(8):
            ref[pl.ds(16 * p + 8 * h + r, BLOCKS, stride=width), :] = blocks[
                BLOCKS * h : BLOCKS * (h + 1), r * SIDE : (r + 1) * SIDE
            ]


def taps_products_kernel(in_ref, there_ref, adjoint_ref, taps_ref, share_ref):
    for h in range(2):
        share_ref[BLOCKS * h : BLOCKS * (h + 1), :] = in_ref[pl.ds(64 + h, BLOCKS, stride=OUT_ROWS), :]
    there = there_ref[...]
    real = imag = 0.0
    for q in range(2):
        xr, xi = points_of(in_ref, there, q)
        gr, gi = points_of(in_ref, there, 2 + q)
        real = real + (xr * gr + xi * gi)
        imag = imag + (xr * gi - xi * gr)
    blocks_of(taps_ref, 0, TAPS_ROWS, adjoint_ref[...], real, imag)


def taps_products(spectra):
    operands = (spectra, jnp.asarray(THERE), jnp.asarray(ADJOINT))
    return call(
        taps_products_kernel, "taps_products", ((BLOCKS * TAPS_ROWS, SIDE), (2 * BLOCKS, SIDE)), operands
    )


def products_kernel(*refs):
    in_ref, shares = refs[0], refs[1 : 1 + CHAN]
    there_ref, back_ref, adjoint_ref, out_ref, taps = refs[1 + CHAN :]
    chan = lax.axis_index("chan")
    for flip in range(CHAN):
        taps[chan ^ flip] = shares[flip][...]
    there, back, adjoint = there_ref[...], back_ref[...], adjoint_ref[...]
    points = dot_wide(there, jnp.concatenate([taps[r] for r in range(8)], axis=1))
    hr, hi = points[:POINTS], points[POINTS:]
    for q in range(2):
        xr, xi = points_of(in_ref, there, q)
        blocks_of(out_ref, q, BACK_ROWS, back, hr * xr - hi * xi, hr * xi + hi * xr)
        gr, gi = points_of(in_ref, there, 2 + q)
        blocks_of(out_ref, 2 + q, BACK_ROWS, adjoint, hr * gr + hi * gi, hr * gi - hi * gr)


def products(spectra, shares):
    operands = (spectra, *shares) + tuple(jnp.asarray(t) for t in (THERE, BACK, ADJOINT))
    scratch = [pltpu.VMEM((CHAN, 2 * BLOCKS, SIDE), jnp.float32)]
    return call(products_kernel, "products", (BLOCKS * BACK_ROWS, SIDE), operands, scratch)


def close(in_ref, inner_ref, outer_ref, twist_ref, gathered, rows, pairs, width):
    count = 2 * len(pairs)
    for p, pair in enumerate(pairs):
        for h in range(2):
            for r in range(8):
                gathered[h, pl.ds(pair[r // SUB] * SIDE + r % SUB, BLOCKS, stride=SUB), :] = in_ref[
                    pl.ds(16 * p + 8 * h + r, BLOCKS, stride=width), :
                ]
    turned = dot_three(jnp.concatenate([gathered[0], gathered[1]], axis=1), inner_ref[...])
    cosine, sine = twist_ref[0], twist_ref[1]
    columns = []
    for i in range(count):
        real = turned[i * SIDE : (i + 1) * SIDE, :SIDE]
        imag = turned[i * SIDE : (i + 1) * SIDE, SIDE:]
        columns.append(jnp.concatenate([real * cosine - imag * sine, imag * cosine + real * sine], axis=0))
    closed = dot_three(outer_ref[...], jnp.concatenate(columns, axis=1))
    for i in range(count):
        rows[i * SIDE : (i + 1) * SIDE, :] = closed[:, i * SIDE : (i + 1) * SIDE]


def taps_kernel(in_ref, inner_ref, outer_ref, twist_ref, f_ref, gathered, rows):
    close(in_ref, inner_ref, outer_ref, twist_ref, gathered, rows, ((0, 1),), TAPS_ROWS)
    for a in range(SIDE):
        f_ref[:, a * SIDE : (a + 1) * SIDE] = rows[pl.ds(a, 2, stride=SIDE), :]


def inverse_kernel(in_ref, seq_ref, cot_ref, skip_ref, inner_ref, outer_ref, twist_ref, y_ref, g_ref, gathered, rows):
    close(in_ref, inner_ref, outer_ref, twist_ref, gathered, rows, PAIRS[:4], BACK_ROWS)
    skip = jnp.broadcast_to(skip_ref[...], (4, SIDE))
    for a in range(SIDE):
        lanes = slice(a * SIDE, (a + 1) * SIDE)
        y_ref[:, lanes] = rows[pl.ds(a, 4, stride=SIDE), :] + skip * seq_ref[:, lanes]
        g_ref[:, lanes] = rows[pl.ds(4 * SIDE + a, 4, stride=SIDE), :] + skip * cot_ref[:, lanes]


def close_scratch(count):
    return [pltpu.VMEM((2, count * SIDE, SIDE), jnp.float32), pltpu.VMEM((count * SIDE, SIDE), jnp.float32)]


def taps_blocks(spectra):
    operands = (spectra,) + tuple(jnp.asarray(t) for t in INVERSE_TABLES)
    return call(taps_kernel, "taps_blocks", (2, BLOCK), operands, close_scratch(2))


def inverse_blocks(spectra, sequence, cotangent, skip_gain):
    operands = (spectra, sequence, cotangent, skip_gain[:, None]) + tuple(jnp.asarray(t) for t in INVERSE_TABLES)
    return call(inverse_kernel, "inverse_blocks", ((4, BLOCK), (4, BLOCK)), operands, close_scratch(8))


def exchange(blocks):
    rows = blocks.shape[0] // BLOCKS
    tall = 1 if rows % 8 else 8
    cut = blocks.reshape(BLOCKS, rows // tall, tall, SIDE)
    return lax.all_to_all(cut, "ctx", split_axis=0, concat_axis=0, tiled=True).reshape(blocks.shape)


def flip_chan(values, flip):
    return lax.ppermute(values, "chan", [(i, i ^ flip) for i in range(CHAN)])


def sum_over_chan(values):
    for flip in (1, 3, 4):
        values = values + flip_chan(values, flip)
    return values


def body(sequence, filter_taps, skip_gain, cotangent):
    spectra = exchange(forward_blocks(sequence, cotangent, filter_taps))
    taps, share = taps_products(spectra)
    taps = exchange(taps)
    shares = [share] + [flip_chan(share, flip) for flip in (1, 2, 3)]
    shares = shares + [flip_chan(s, 4) for s in shares]
    back = products(spectra, shares)
    taps, back = lax.optimization_barrier((taps, back))
    taps_grad = sum_over_chan(taps_blocks(taps))
    convolved, seq_grad = inverse_blocks(exchange(back), sequence, cotangent, skip_gain)
    return convolved, seq_grad, taps_grad


def solution(mesh):
    return jax.shard_map(
        body,
        mesh=mesh,
        in_specs=(P("chan", "ctx"), P(None, "ctx"), P("chan"), P("chan", "ctx")),
        out_specs=(P("chan", "ctx"), P("chan", "ctx"), P(None, "ctx")),
        check_vma=False,
    )
```

```python
import numpy as np
import jax
import jax.numpy as jnp
from jax import lax
from jax.experimental import pallas as pl
from jax.experimental.pallas import tpu as pltpu
from jax.sharding import PartitionSpec as P

SIDE = 128
BLOCK = SIDE * SIDE
BLOCKS = 32
SUB = SIDE // BLOCKS
POINTS = 2 * BLOCKS
CHAN = 8
HALF = 4
OUT_ROWS = 72
BACK_ROWS = 64
TAPS_ROWS = 16
PAIRS = ((0, 2), (1, 3), (4, 6), (5, 7), (8, 9))
VMEM_LIMIT = 40 * 1024 * 1024
VMEM_FULL = 60 * 1024 * 1024


def make_tables():
    digit = np.arange(SIDE)
    turn = 2.0 * np.pi
    single = np.float32
    angle = turn * ((digit[:, None] + 0.25) * digit[None, :] / SIDE)
    cosine, sine = np.cos(angle), np.sin(angle)
    forward_outer = np.concatenate([cosine, -sine], axis=0)
    factor = (BLOCKS * BLOCK) ** (-0.5) / BLOCK
    row = np.arange(2 * SIDE)
    coarse, signal = SUB * (row // (2 * SUB)) + row % SUB, (row // SUB) % 2
    own = signal[None, :] == np.arange(2)[:, None]
    pair_cosine = (own[:, None, :] * cosine[coarse].T[None]).reshape(2 * SIDE, 2 * SIDE)
    pair_sine = (own[:, None, :] * sine[coarse].T[None]).reshape(2 * SIDE, 2 * SIDE)
    inverse_outer = factor * np.concatenate([pair_cosine, -pair_sine], axis=1)
    angle = turn * ((digit[:, None] + 0.25) * digit[None, :] / BLOCK)
    twist = np.stack([np.cos(angle), np.sin(angle)])
    angle = turn * ((digit[:, None] * digit[None, :]) % SIDE / SIDE)
    cosine, sine = np.cos(angle), np.sin(angle)
    forward_inner = np.block([[cosine, -sine], [sine, cosine]])
    inverse_inner = np.block([[cosine, sine], [-sine, cosine]])
    return (
        tuple(t.astype(single) for t in (forward_outer, forward_inner, twist)),
        tuple(t.astype(single) for t in (inverse_inner, inverse_outer, twist[:, coarse])),
    )


def make_block_tables():
    block = np.arange(BLOCKS)
    point = np.arange(POINTS)
    angle = 2.0 * np.pi * ((point[:, None] * block[None, :]) % POINTS) / POINTS
    cosine, sine = np.cos(angle), np.sin(angle)
    tables = [np.block([[cosine, sine], [-sine, cosine]])]
    step = np.exp(-2j * np.pi * point / POINTS)
    for spill in (1.0 + 1j * step, 1.0 - 1j * np.conj(step)):
        back = np.exp(1j * angle.T) * spill[None, :] / POINTS
        tables.append(np.block([[back.real, -back.imag], [back.imag, back.real]]))
    return tuple(t.astype(np.float32) for t in tables)


FORWARD_TABLES, INVERSE_TABLES = make_tables()
THERE, BACK, ADJOINT = make_block_tables()


def split(values):
    high = values.astype(jnp.bfloat16)
    return high, (values - high.astype(jnp.float32)).astype(jnp.bfloat16)


def dot(left, right):
    return jnp.dot(left, right, preferred_element_type=jnp.float32)


def dot_three(left, right):
    (lh, ll), (rh, rl) = split(left), split(right)
    return dot(lh, rh) + (dot(lh, rl) + dot(ll, rh))


def dot_wide(left, right):
    (lh, ll), (rh, rl) = split(left), split(right)
    return dot(jnp.concatenate([lh, lh, ll], axis=1), jnp.concatenate([rh, rl, rh], axis=0))


def call(kernel, name, out_shape, operands, scratch=(), own_copies=False):
    space = pl.ANY if own_copies else pltpu.VMEM
    many = isinstance(out_shape[0], tuple)
    shapes = tuple(jax.ShapeDtypeStruct(s, jnp.float32) for s in (out_shape if many else (out_shape,)))
    outs = (pl.BlockSpec(memory_space=pltpu.VMEM),) * len(shapes)
    return pl.pallas_call(
        kernel,
        out_shape=shapes if many else shapes[0],
        in_specs=[pl.BlockSpec(memory_space=space)] * len(operands),
        out_specs=outs if many else outs[0],
        scratch_shapes=list(scratch),
        compiler_params=pltpu.CompilerParams(vmem_limit_bytes=VMEM_FULL if own_copies else VMEM_LIMIT),
        name=name,
    )(*operands)


def spread(source, rows, first, count):
    for a in range(SIDE):
        rows[pl.ds(first * SIDE + a, count, stride=SIDE), :] = source[:, a * SIDE : (a + 1) * SIDE]


def forward_kernel(*refs):
    sources, out_ref, held, rows, spectra, sems = refs[:6], refs[6], refs[7:13], refs[13], refs[14], refs[15]
    copies = [pltpu.make_async_copy(s, h, sems.at[i]) for i, (s, h) in enumerate(zip(sources, held))]
    for copy in copies:
        copy.start()
    seq_ref, cot_ref, taps_ref, outer_ref, inner_ref, twist_ref = held
    copies[0].wait()
    spread(seq_ref, rows, 0, 4)
    copies[1].wait()
    spread(cot_ref, rows, 4, 4)
    copies[2].wait()
    spread(taps_ref, rows, 8, 2)
    for copy in copies[3:]:
        copy.wait()

    signals = jnp.concatenate([rows[i * SIDE : (i + 1) * SIDE, :] for i in range(10)], axis=1)
    opened = dot_wide(outer_ref[...], signals)
    cosine, sine = twist_ref[0], twist_ref[1]
    inner = inner_ref[...]
    half = lax.axis_index("chan") // HALF
    for p, pair in enumerate(PAIRS):
        twisted = []
        for i in pair:
            real = opened[:SIDE, i * SIDE : (i + 1) * SIDE]
            imag = opened[SIDE:, i * SIDE : (i + 1) * SIDE]
            twisted.append(jnp.concatenate([real * cosine + imag * sine, imag * cosine - real * sine], axis=1))
        spectrum = dot_three(jnp.concatenate(twisted, axis=0), inner)
        for h in range(2):
            held_rows = spectra.at[2 * p + h]
            held_rows[...] = spectrum[:, h * SIDE : (h + 1) * SIDE]
            picked = [held_rows[pl.ds((r // SUB) * SIDE + r % SUB, BLOCKS, stride=SUB), :] for r in range(8)]
            if p < 4:
                for r in range(8):
                    out_ref[pl.ds(16 * p + 8 * h + r, BLOCKS, stride=OUT_ROWS), :] = picked[r]
            else:
                for r in range(SUB):
                    out_ref[pl.ds(64 + SUB * h + r, BLOCKS, stride=OUT_ROWS), :] = jnp.where(
                        half == 0, picked[r], picked[SUB + r]
                    )


def forward_blocks(sequence, cotangent, taps):
    operands = (sequence, cotangent, taps) + tuple(jnp.asarray(t) for t in FORWARD_TABLES)
    scratch = [pltpu.VMEM(v.shape, v.dtype) for v in operands] + [
        pltpu.VMEM((10 * SIDE, SIDE), jnp.float32),
        pltpu.VMEM((10, 2 * SIDE, SIDE), jnp.float32),
        pltpu.SemaphoreType.DMA((6,)),
    ]
    return call(forward_kernel, "forward_blocks", (BLOCKS * OUT_ROWS, SIDE), operands, scratch, True)


def points_of(in_ref, there, p):
    halves = [
        jnp.concatenate(
            [in_ref[pl.ds(16 * p + 8 * h + r, BLOCKS, stride=OUT_ROWS), :] for r in range(8)], axis=1
        )
        for h in range(2)
    ]
    points = dot_wide(there, jnp.concatenate(halves, axis=0))
    return points[:POINTS], points[POINTS:]


def blocks_of(ref, p, width, table, real, imag):
    blocks = dot_wide(table, jnp.concatenate([real, imag], axis=0))
    for h in range(2):
        for r in range(8):
            ref[pl.ds(16 * p + 8 * h + r, BLOCKS, stride=width), :] = blocks[
                BLOCKS * h : BLOCKS * (h + 1), r * SIDE : (r + 1) * SIDE
            ]


def taps_products_kernel(in_ref, there_ref, adjoint_ref, taps_ref, share_ref):
    for r in range(8):
        share_ref[BLOCKS * r : BLOCKS * (r + 1), :] = in_ref[pl.ds(64 + r, BLOCKS, stride=OUT_ROWS), :]
    there = there_ref[...]
    real = imag = 0.0
    for q in range(2):
        xr, xi = points_of(in_ref, there, q)
        gr, gi = points_of(in_ref, there, 2 + q)
        real = real + (xr * gr + xi * gi)
        imag = imag + (xr * gi - xi * gr)
    blocks_of(taps_ref, 0, TAPS_ROWS, adjoint_ref[...], real, imag)


def taps_products(spectra):
    operands = (spectra, jnp.asarray(THERE), jnp.asarray(ADJOINT))
    return call(
        taps_products_kernel, "taps_products", ((BLOCKS * TAPS_ROWS, SIDE), (8 * BLOCKS, SIDE)), operands
    )


def products_kernel(in_ref, own_ref, other_ref, there_ref, back_ref, adjoint_ref, out_ref):
    half = lax.axis_index("chan") // HALF
    there, back, adjoint = there_ref[...], back_ref[...], adjoint_ref[...]

    def taps_row(f, h, c):
        lines = slice(BLOCKS * (SUB * h + c), BLOCKS * (SUB * h + c + 1))
        return jnp.where(half == f, own_ref[lines, :], other_ref[lines, :])

    halves = [
        jnp.concatenate([taps_row(f, h, c) for f in range(2) for c in range(SUB)], axis=1) for h in range(2)
    ]
    points = dot_wide(there, jnp.concatenate(halves, axis=0))
    hr, hi = points[:POINTS], points[POINTS:]
    for q in range(2):
        xr, xi = points_of(in_ref, there, q)
        blocks_of(out_ref, q, BACK_ROWS, back, hr * xr - hi * xi, hr * xi + hi * xr)
        gr, gi = points_of(in_ref, there, 2 + q)
        blocks_of(out_ref, 2 + q, BACK_ROWS, adjoint, hr * gr + hi * gi, hr * gi - hi * gr)


def products(spectra, own, other):
    operands = (spectra, own, other) + tuple(jnp.asarray(t) for t in (THERE, BACK, ADJOINT))
    return call(products_kernel, "products", (BLOCKS * BACK_ROWS, SIDE), operands)


def close(in_ref, inner_ref, outer_ref, twist_ref, rows, places):
    cosine, sine = twist_ref[0], twist_ref[1]
    inner = inner_ref[...]
    columns = []
    for p in range(len(places)):
        both = jnp.concatenate(
            [in_ref[:, 16 * p + 8 * h : 16 * p + 8 * h + 8, :].reshape(2 * SIDE, SIDE) for h in range(2)], axis=1
        )
        turned = dot_three(both, inner)
        real, imag = turned[:, :SIDE], turned[:, SIDE:]
        columns.append(jnp.concatenate([real * cosine - imag * sine, imag * cosine + real * sine], axis=0))
    closed = dot_three(outer_ref[...], jnp.concatenate(columns, axis=1))
    for p, pair in enumerate(places):
        for half, place in enumerate(pair):
            rows[place * SIDE : (place + 1) * SIDE, :] = closed[
                half * SIDE : (half + 1) * SIDE, p * SIDE : (p + 1) * SIDE
            ]


def taps_kernel(in_ref, inner_ref, outer_ref, twist_ref, f_ref, rows):
    close(in_ref, inner_ref, outer_ref, twist_ref, rows, ((0, 1),))
    for a in range(SIDE):
        f_ref[:, a * SIDE : (a + 1) * SIDE] = rows[pl.ds(a, 2, stride=SIDE), :]


def inverse_kernel(in_ref, seq_ref, cot_ref, skip_ref, inner_ref, outer_ref, twist_ref, y_ref, g_ref, rows):
    close(in_ref, inner_ref, outer_ref, twist_ref, rows, PAIRS[:4])
    skip = jnp.broadcast_to(skip_ref[...], (4, SIDE))
    for a in range(SIDE):
        lanes = slice(a * SIDE, (a + 1) * SIDE)
        y_ref[:, lanes] = rows[pl.ds(a, 4, stride=SIDE), :] + skip * seq_ref[:, lanes]
        g_ref[:, lanes] = rows[pl.ds(4 * SIDE + a, 4, stride=SIDE), :] + skip * cot_ref[:, lanes]


def taps_blocks(spectra):
    operands = (spectra,) + tuple(jnp.asarray(t) for t in INVERSE_TABLES)
    return call(taps_kernel, "taps_blocks", (2, BLOCK), operands, [pltpu.VMEM((2 * SIDE, SIDE), jnp.float32)])


def inverse_blocks(spectra, sequence, cotangent, skip_gain):
    operands = (spectra, sequence, cotangent, skip_gain[:, None]) + tuple(jnp.asarray(t) for t in INVERSE_TABLES)
    scratch = [pltpu.VMEM((8 * SIDE, SIDE), jnp.float32)]
    return call(inverse_kernel, "inverse_blocks", ((4, BLOCK), (4, BLOCK)), operands, scratch)


def exchange(blocks):
    cut = blocks.reshape(BLOCKS, -1, SIDE)
    return lax.all_to_all(cut, "ctx", split_axis=0, concat_axis=0, tiled=True)


def flip_chan(values, flip):
    return lax.ppermute(values, "chan", [(i, i ^ flip) for i in range(CHAN)])


def sum_over_chan(values):
    for flip in (1, 3, 4):
        values = values + flip_chan(values, flip)
    return values


def body(sequence, filter_taps, skip_gain, cotangent):
    spectra = exchange(forward_blocks(sequence, cotangent, filter_taps)).reshape(BLOCKS * OUT_ROWS, SIDE)
    taps, share = taps_products(spectra)
    taps = exchange(taps)
    back = products(spectra, share, flip_chan(share, HALF))
    taps, back = lax.optimization_barrier((taps, back))
    taps_grad = sum_over_chan(taps_blocks(taps))
    convolved, seq_grad = inverse_blocks(exchange(back), sequence, cotangent, skip_gain)
    return convolved, seq_grad, taps_grad


def solution(mesh):
    return jax.shard_map(
        body,
        mesh=mesh,
        in_specs=(P("chan", "ctx"), P(None, "ctx"), P("chan"), P("chan", "ctx")),
        out_specs=(P("chan", "ctx"), P("chan", "ctx"), P(None, "ctx")),
        check_vma=False,
    )
```

```python
import numpy as np
import jax
import jax.numpy as jnp
from jax import lax
from jax.experimental import pallas as pl
from jax.experimental.pallas import tpu as pltpu
from jax.sharding import PartitionSpec as P

SIDE = 128
BLOCK = SIDE * SIDE
BLOCKS = 32
SUB = SIDE // BLOCKS
POINTS = 2 * BLOCKS
CHAN = 8
OUT_ROWS = 80
BACK_ROWS = 64
TAPS_ROWS = 16
PAIRS = ((0, 2), (1, 3), (4, 6), (5, 7), (8, 9))
VMEM_LIMIT = 40 * 1024 * 1024
VMEM_FULL = 60 * 1024 * 1024


def make_tables():
    digit = np.arange(SIDE)
    turn = 2.0 * np.pi
    single = np.float32
    angle = turn * ((digit[:, None] + 0.25) * digit[None, :] / SIDE)
    cosine, sine = np.cos(angle), np.sin(angle)
    forward_outer = np.concatenate([cosine, -sine], axis=0)
    factor = (BLOCKS * BLOCK) ** (-0.5) / BLOCK
    row = np.arange(2 * SIDE)
    coarse, signal = SUB * (row // (2 * SUB)) + row % SUB, (row // SUB) % 2
    own = signal[None, :] == np.arange(2)[:, None]
    pair_cosine = (own[:, None, :] * cosine[coarse].T[None]).reshape(2 * SIDE, 2 * SIDE)
    pair_sine = (own[:, None, :] * sine[coarse].T[None]).reshape(2 * SIDE, 2 * SIDE)
    inverse_outer = factor * np.concatenate([pair_cosine, -pair_sine], axis=1)
    angle = turn * ((digit[:, None] + 0.25) * digit[None, :] / BLOCK)
    twist = np.stack([np.cos(angle), np.sin(angle)])
    angle = turn * ((digit[:, None] * digit[None, :]) % SIDE / SIDE)
    cosine, sine = np.cos(angle), np.sin(angle)
    forward_inner = np.block([[cosine, -sine], [sine, cosine]])
    inverse_inner = np.block([[cosine, sine], [-sine, cosine]])
    return (
        tuple(t.astype(single) for t in (forward_outer, forward_inner, twist)),
        tuple(t.astype(single) for t in (inverse_inner, inverse_outer, twist[:, coarse])),
    )


def make_block_tables():
    block = np.arange(BLOCKS)
    point = np.arange(POINTS)
    angle = 2.0 * np.pi * ((point[:, None] * block[None, :]) % POINTS) / POINTS
    cosine, sine = np.cos(angle), np.sin(angle)
    tables = [np.block([[cosine, sine], [-sine, cosine]])]
    step = np.exp(-2j * np.pi * point / POINTS)
    for spill in (1.0 + 1j * step, 1.0 - 1j * np.conj(step)):
        back = np.exp(1j * angle.T) * spill[None, :] / POINTS
        tables.append(np.block([[back.real, -back.imag], [back.imag, back.real]]))
    return tuple(t.astype(np.float32) for t in tables)


FORWARD_TABLES, INVERSE_TABLES = make_tables()
THERE, BACK, ADJOINT = make_block_tables()


def split(values):
    high = values.astype(jnp.bfloat16)
    return high, (values - high.astype(jnp.float32)).astype(jnp.bfloat16)


def dot(left, right):
    return jnp.dot(left, right, preferred_element_type=jnp.float32)


def dot_three(left, right):
    (lh, ll), (rh, rl) = split(left), split(right)
    return dot(lh, rh) + (dot(lh, rl) + dot(ll, rh))


def dot_wide(left, right):
    (lh, ll), (rh, rl) = split(left), split(right)
    return dot(jnp.concatenate([lh, lh, ll], axis=1), jnp.concatenate([rh, rl, rh], axis=0))


def call(kernel, name, out_shape, operands, scratch=(), own_copies=False):
    space = pl.ANY if own_copies else pltpu.VMEM
    many = isinstance(out_shape[0], tuple)
    shapes = tuple(jax.ShapeDtypeStruct(s, jnp.float32) for s in (out_shape if many else (out_shape,)))
    outs = (pl.BlockSpec(memory_space=space),) * len(shapes)
    return pl.pallas_call(
        kernel,
        out_shape=shapes if many else shapes[0],
        in_specs=[pl.BlockSpec(memory_space=space)] * len(operands),
        out_specs=outs if many else outs[0],
        scratch_shapes=list(scratch),
        compiler_params=pltpu.CompilerParams(vmem_limit_bytes=VMEM_FULL if own_copies else VMEM_LIMIT),
        name=name,
    )(*operands)


def spread(source, rows, first, count):
    for a in range(SIDE):
        rows[pl.ds(first * SIDE + a, count, stride=SIDE), :] = source[:, a * SIDE : (a + 1) * SIDE]


def forward_kernel(*refs):
    sources, out_ref, held, rows, sent, sems = refs[:6], refs[6], refs[7:13], refs[13], refs[14], refs[15]
    copies = [pltpu.make_async_copy(s, h, sems.at[i]) for i, (s, h) in enumerate(zip(sources, held))]
    for copy in copies:
        copy.start()
    seq_ref, cot_ref, taps_ref, outer_ref, inner_ref, twist_ref = held
    copies[0].wait()
    spread(seq_ref, rows, 0, 4)
    copies[1].wait()
    spread(cot_ref, rows, 4, 4)
    copies[2].wait()
    spread(taps_ref, rows, 8, 2)
    for copy in copies[3:]:
        copy.wait()

    signals = jnp.concatenate([rows[i * SIDE : (i + 1) * SIDE, :] for i in range(10)], axis=1)
    opened = dot_wide(outer_ref[...], signals)
    cosine, sine = twist_ref[0], twist_ref[1]
    inner = inner_ref[...]
    low = lax.broadcasted_iota(jnp.int32, (SIDE // 8, 8, SIDE), 1) < SUB
    leaving = []
    for p, pair in enumerate(PAIRS):
        twisted = []
        for i in pair:
            real = opened[:SIDE, i * SIDE : (i + 1) * SIDE]
            imag = opened[SIDE:, i * SIDE : (i + 1) * SIDE]
            twisted.append(jnp.concatenate([real * cosine + imag * sine, imag * cosine - real * sine], axis=1))
        spectrum = dot_three(jnp.concatenate(twisted, axis=0), inner)
        for h in range(2):
            first, second = (
                spectrum[i * SIDE : (i + 1) * SIDE, h * SIDE : (h + 1) * SIDE].reshape(SIDE // 8, 8, SIDE)
                for i in range(2)
            )
            sent[p, :, 0, 8 * h : 8 * h + 8, :] = jnp.where(low, first, pltpu.roll(second, SUB, 1))
            sent[p, :, 1, 8 * h : 8 * h + 8, :] = jnp.where(low, pltpu.roll(first, SUB, 1), second)
        copy = pltpu.make_async_copy(sent.at[p], out_ref.at[:, :, 16 * p : 16 * p + 16, :], sems.at[6 + p])
        copy.start()
        leaving.append(copy)
    for copy in leaving:
        copy.wait()


def forward_blocks(sequence, cotangent, taps):
    operands = (sequence, cotangent, taps) + tuple(jnp.asarray(t) for t in FORWARD_TABLES)
    scratch = [pltpu.VMEM(v.shape, v.dtype) for v in operands] + [
        pltpu.VMEM((10 * SIDE, SIDE), jnp.float32),
        pltpu.VMEM((5, BLOCKS // 2, 2, 16, SIDE), jnp.float32),
        pltpu.SemaphoreType.DMA((11,)),
    ]
    shape = (BLOCKS // 2, 2, OUT_ROWS, SIDE)
    return call(forward_kernel, "forward_blocks", shape, operands, scratch, True)


def points_of(in_ref, there, p):
    halves = [
        jnp.concatenate(
            [in_ref[pl.ds(16 * p + 8 * h + r, BLOCKS, stride=OUT_ROWS), :] for r in range(8)], axis=1
        )
        for h in range(2)
    ]
    points = dot_wide(there, jnp.concatenate(halves, axis=0))
    return points[:POINTS], points[POINTS:]


def blocks_of(ref, p, width, table, real, imag):
    blocks = dot_wide(table, jnp.concatenate([real, imag], axis=0))
    for h in range(2):
        for r in range(8):
            ref[pl.ds(16 * p + 8 * h + r, BLOCKS, stride=width), :] = blocks[
                BLOCKS * h : BLOCKS * (h + 1), r * SIDE : (r + 1) * SIDE
            ]


def taps_products_kernel(in_ref, there_ref, adjoint_ref, taps_ref):
    there = there_ref[...]
    real = imag = 0.0
    for q in range(2):
        xr, xi = points_of(in_ref, there, q)
        gr, gi = points_of(in_ref, there, 2 + q)
        real = real + (xr * gr + xi * gi)
        imag = imag + (xr * gi - xi * gr)
    blocks_of(taps_ref, 0, TAPS_ROWS, adjoint_ref[...], real, imag)


def taps_products(spectra):
    operands = (spectra, jnp.asarray(THERE), jnp.asarray(ADJOINT))
    return call(taps_products_kernel, "taps_products", (BLOCKS * TAPS_ROWS, SIDE), operands)


def products_kernel(in_ref, there_ref, back_ref, adjoint_ref, out_ref):
    there, back, adjoint = there_ref[...], back_ref[...], adjoint_ref[...]
    hr, hi = points_of(in_ref, there, 4)
    for q in range(2):
        xr, xi = points_of(in_ref, there, q)
        blocks_of(out_ref, q, BACK_ROWS, back, hr * xr - hi * xi, hr * xi + hi * xr)
        gr, gi = points_of(in_ref, there, 2 + q)
        blocks_of(out_ref, 2 + q, BACK_ROWS, adjoint, hr * gr + hi * gi, hr * gi - hi * gr)


def products(spectra):
    operands = (spectra,) + tuple(jnp.asarray(t) for t in (THERE, BACK, ADJOINT))
    return call(products_kernel, "products", (BLOCKS * BACK_ROWS, SIDE), operands)


def close(in_ref, inner_ref, outer_ref, twist_ref, rows, places):
    cosine, sine = twist_ref[0], twist_ref[1]
    inner = inner_ref[...]
    columns = []
    for p in range(len(places)):
        both = jnp.concatenate(
            [in_ref[:, 16 * p + 8 * h : 16 * p + 8 * h + 8, :].reshape(2 * SIDE, SIDE) for h in range(2)], axis=1
        )
        turned = dot_three(both, inner)
        real, imag = turned[:, :SIDE], turned[:, SIDE:]
        columns.append(jnp.concatenate([real * cosine - imag * sine, imag * cosine + real * sine], axis=0))
    closed = dot_three(outer_ref[...], jnp.concatenate(columns, axis=1))
    for p, pair in enumerate(places):
        for half, place in enumerate(pair):
            rows[place * SIDE : (place + 1) * SIDE, :] = closed[
                half * SIDE : (half + 1) * SIDE, p * SIDE : (p + 1) * SIDE
            ]


def taps_kernel(in_ref, inner_ref, outer_ref, twist_ref, f_ref, rows):
    close(in_ref, inner_ref, outer_ref, twist_ref, rows, ((0, 1),))
    for a in range(SIDE):
        f_ref[:, a * SIDE : (a + 1) * SIDE] = rows[pl.ds(a, 2, stride=SIDE), :]


def inverse_kernel(in_ref, seq_ref, cot_ref, skip_ref, inner_ref, outer_ref, twist_ref, y_ref, g_ref, rows):
    close(in_ref, inner_ref, outer_ref, twist_ref, rows, PAIRS[:4])
    skip = jnp.broadcast_to(skip_ref[...], (4, SIDE))
    for a in range(SIDE):
        lanes = slice(a * SIDE, (a + 1) * SIDE)
        y_ref[:, lanes] = rows[pl.ds(a, 4, stride=SIDE), :] + skip * seq_ref[:, lanes]
        g_ref[:, lanes] = rows[pl.ds(4 * SIDE + a, 4, stride=SIDE), :] + skip * cot_ref[:, lanes]


def taps_blocks(spectra):
    operands = (spectra,) + tuple(jnp.asarray(t) for t in INVERSE_TABLES)
    return call(taps_kernel, "taps_blocks", (2, BLOCK), operands, [pltpu.VMEM((2 * SIDE, SIDE), jnp.float32)])


def inverse_blocks(spectra, sequence, cotangent, skip_gain):
    operands = (spectra, sequence, cotangent, skip_gain[:, None]) + tuple(jnp.asarray(t) for t in INVERSE_TABLES)
    scratch = [pltpu.VMEM((8 * SIDE, SIDE), jnp.float32)]
    return call(inverse_kernel, "inverse_blocks", ((4, BLOCK), (4, BLOCK)), operands, scratch)


def exchange(blocks):
    cut = blocks.reshape(BLOCKS, -1, SIDE)
    return lax.all_to_all(cut, "ctx", split_axis=0, concat_axis=0, tiled=True)


def flip_chan(values, flip):
    return lax.ppermute(values, "chan", [(i, i ^ flip) for i in range(CHAN)])


def sum_over_chan(values):
    for flip in (1, 3, 4):
        values = values + flip_chan(values, flip)
    return values


def body(sequence, filter_taps, skip_gain, cotangent):
    spectra = exchange(forward_blocks(sequence, cotangent, filter_taps)).reshape(BLOCKS * OUT_ROWS, SIDE)
    taps = exchange(taps_products(spectra))
    back = products(spectra)
    taps, back = lax.optimization_barrier((taps, back))
    taps_grad = sum_over_chan(taps_blocks(taps))
    convolved, seq_grad = inverse_blocks(exchange(back), sequence, cotangent, skip_gain)
    return convolved, seq_grad, taps_grad


def solution(mesh):
    return jax.shard_map(
        body,
        mesh=mesh,
        in_specs=(P("chan", "ctx"), P(None, "ctx"), P("chan"), P("chan", "ctx")),
        out_specs=(P("chan", "ctx"), P("chan", "ctx"), P(None, "ctx")),
        check_vma=False,
    )
```

```python
import numpy as np
import jax
import jax.numpy as jnp
from jax import lax
from jax.experimental import pallas as pl
from jax.experimental.pallas import tpu as pltpu
from jax.sharding import PartitionSpec as P

SIDE = 128
BLOCK = SIDE * SIDE
BLOCKS = 32
SUB = SIDE // BLOCKS
POINTS = 2 * BLOCKS
CHAN = 8
OUT_ROWS = 80
BACK_ROWS = 64
PAIRS = ((0, 2), (1, 3), (4, 6), (5, 7), (8, 9))
VMEM_LIMIT = 40 * 1024 * 1024


def make_tables():
    digit = np.arange(SIDE)
    turn = 2.0 * np.pi
    single = np.float32
    angle = turn * ((digit[:, None] + 0.25) * digit[None, :] / SIDE)
    cosine, sine = np.cos(angle), np.sin(angle)
    forward_outer = np.concatenate([cosine, -sine], axis=0)
    factor = (BLOCKS * BLOCK) ** (-0.5) / BLOCK
    row = np.arange(2 * SIDE)
    coarse, signal = SUB * (row // (2 * SUB)) + row % SUB, (row // SUB) % 2
    own = signal[None, :] == np.arange(2)[:, None]
    pair_cosine = (own[:, None, :] * cosine[coarse].T[None]).reshape(2 * SIDE, 2 * SIDE)
    pair_sine = (own[:, None, :] * sine[coarse].T[None]).reshape(2 * SIDE, 2 * SIDE)
    inverse_outer = factor * np.concatenate([pair_cosine, -pair_sine], axis=1)
    angle = turn * ((digit[:, None] + 0.25) * digit[None, :] / BLOCK)
    twist = np.stack([np.cos(angle), np.sin(angle)])
    angle = turn * ((digit[:, None] * digit[None, :]) % SIDE / SIDE)
    cosine, sine = np.cos(angle), np.sin(angle)
    forward_inner = np.block([[cosine, -sine], [sine, cosine]])
    inverse_inner = np.block([[cosine, sine], [-sine, cosine]])
    return (
        np.stack([forward_outer, forward_inner[:, :SIDE], forward_inner[:, SIDE:]]).astype(single),
        tuple(t.astype(single) for t in (inverse_inner, inverse_outer, twist[:, coarse])),
    )


def make_block_tables():
    block = np.arange(BLOCKS)
    point = np.arange(POINTS)
    angle = 2.0 * np.pi * ((point[:, None] * block[None, :]) % POINTS) / POINTS
    cosine, sine = np.cos(angle), np.sin(angle)
    tables = [np.block([[cosine, sine], [-sine, cosine]])]
    step = np.exp(-2j * np.pi * point / POINTS)
    for spill in (1.0 + 1j * step, 1.0 - 1j * np.conj(step)):
        back = np.exp(1j * angle.T) * spill[None, :] / POINTS
        tables.append(np.block([[back.real, -back.imag], [back.imag, back.real]]))
    return tuple(t.astype(np.float32) for t in tables)


FORWARD_TABLES, INVERSE_TABLES = make_tables()
THERE, BACK, ADJOINT = make_block_tables()


def split(values):
    high = values.astype(jnp.bfloat16)
    return high, (values - high.astype(jnp.float32)).astype(jnp.bfloat16)


def dot(left, right):
    return jnp.dot(left, right, preferred_element_type=jnp.float32)


def dot_three(left, right):
    (lh, ll), (rh, rl) = split(left), split(right)
    return dot(lh, rh) + (dot(lh, rl) + dot(ll, rh))


def dot_wide(left, right):
    (lh, ll), (rh, rl) = split(left), split(right)
    return dot(jnp.concatenate([lh, lh, ll], axis=1), jnp.concatenate([rh, rl, rh], axis=0))


def call(kernel, name, out_shape, operands, scratch=()):
    many = isinstance(out_shape[0], tuple)
    shapes = tuple(jax.ShapeDtypeStruct(s, jnp.float32) for s in (out_shape if many else (out_shape,)))
    outs = (pl.BlockSpec(memory_space=pltpu.VMEM),) * len(shapes)
    return pl.pallas_call(
        kernel,
        out_shape=shapes if many else shapes[0],
        in_specs=[pl.BlockSpec(memory_space=pltpu.VMEM)] * len(operands),
        out_specs=outs if many else outs[0],
        scratch_shapes=list(scratch),
        compiler_params=pltpu.CompilerParams(vmem_limit_bytes=VMEM_LIMIT),
        name=name,
    )(*operands)


def spread(source, rows, first, count):
    for a in range(SIDE):
        rows[pl.ds(first * SIDE + a, count, stride=SIDE), :] = source[:, a * SIDE : (a + 1) * SIDE]


def twist_kernel(twist_ref):
    c = lax.broadcasted_iota(jnp.int32, (SIDE, SIDE), 0).astype(jnp.float32)
    b = lax.broadcasted_iota(jnp.int32, (SIDE, SIDE), 1).astype(jnp.float32)
    angle = (c + 0.25) * b * (2.0 * np.pi / BLOCK)
    twist_ref[0] = jnp.cos(angle)
    twist_ref[1] = jnp.sin(angle)


def twist_table():
    return pl.pallas_call(
        twist_kernel,
        out_shape=jax.ShapeDtypeStruct((2, SIDE, SIDE), jnp.float32),
        out_specs=pl.BlockSpec(memory_space=pltpu.VMEM),
        compiler_params=pltpu.CompilerParams(vmem_limit_bytes=4 * 1024 * 1024),
        cost_estimate=pl.CostEstimate(flops=4_000_000_000, bytes_accessed=8_000_000, transcendentals=32768),
        name="twist_table",
    )()


def forward_kernel(seq_ref, cot_ref, taps_ref, tables_ref, twist_ref, out_ref, rows):
    spread(seq_ref, rows, 0, 4)
    spread(cot_ref, rows, 4, 4)
    spread(taps_ref, rows, 8, 2)

    signals = jnp.concatenate([rows[i * SIDE : (i + 1) * SIDE, :] for i in range(10)], axis=1)
    opened = dot_wide(tables_ref[0], signals)
    cosine, sine = twist_ref[0], twist_ref[1]
    inner = jnp.concatenate([tables_ref[1], tables_ref[2]], axis=1)
    low = lax.broadcasted_iota(jnp.int32, (SIDE // 8, 8, SIDE), 1) < SUB
    for p, pair in enumerate(PAIRS):
        twisted = []
        for i in pair:
            real = opened[:SIDE, i * SIDE : (i + 1) * SIDE]
            imag = opened[SIDE:, i * SIDE : (i + 1) * SIDE]
            twisted.append(jnp.concatenate([real * cosine + imag * sine, imag * cosine - real * sine], axis=1))
        spectrum = dot_three(jnp.concatenate(twisted, axis=0), inner)
        for h in range(2):
            first, second = (
                spectrum[i * SIDE : (i + 1) * SIDE, h * SIDE : (h + 1) * SIDE].reshape(SIDE // 8, 8, SIDE)
                for i in range(2)
            )
            lines = slice(16 * p + 8 * h, 16 * p + 8 * h + 8)
            out_ref[:, 0, lines, :] = jnp.where(low, first, pltpu.roll(second, SUB, 1))
            out_ref[:, 1, lines, :] = jnp.where(low, pltpu.roll(first, SUB, 1), second)


def forward_blocks(sequence, cotangent, taps):
    operands = (sequence, cotangent, taps, jnp.asarray(FORWARD_TABLES), twist_table())
    scratch = [pltpu.VMEM((10 * SIDE, SIDE), jnp.float32)]
    return call(forward_kernel, "forward_blocks", (BLOCKS // 2, 2, OUT_ROWS, SIDE), operands, scratch)


def stacked(table):
    high, low = split(table)
    return jnp.concatenate(
        [jnp.concatenate([high, high], axis=1), jnp.concatenate([low, jnp.zeros_like(low)], axis=1)], axis=0
    )


def dot_stacked(left, right):
    both = dot(left, jnp.concatenate(split(right), axis=0))
    half = both.shape[0] // 2
    return both[:half] + both[half:]


def points_of(in_ref, there, p):
    halves = [
        jnp.concatenate(
            [in_ref[pl.ds(16 * p + 8 * h + r, BLOCKS, stride=OUT_ROWS), :] for r in range(8)], axis=1
        )
        for h in range(2)
    ]
    points = dot_wide(there, jnp.concatenate(halves, axis=0))
    return points[:POINTS], points[POINTS:]


def blocks_of(ref, table, real, imag):
    blocks = dot_stacked(table, jnp.concatenate([real, imag], axis=0))
    for h in range(2):
        for r in range(8):
            ref[pl.ds(8 * h + r, BLOCKS, stride=16), :] = blocks[
                BLOCKS * h : BLOCKS * (h + 1), r * SIDE : (r + 1) * SIDE
            ]


def middle_kernel(in_ref, there_ref, back_ref, adjoint_ref, out_ref, taps_ref, sent, sems):
    there, back, adjoint = there_ref[...], stacked(back_ref[...]), stacked(adjoint_ref[...])
    leaving = []

    def leave(p, table, real, imag):
        blocks_of(sent.at[p].reshape(BLOCKS * 16, SIDE), table, real, imag)
        copy = pltpu.make_async_copy(sent.at[p], out_ref.at[:, 16 * p : 16 * p + 16, :], sems.at[p])
        copy.start()
        leaving.append(copy)

    hr, hi = points_of(in_ref, there, 4)
    real = imag = 0.0
    for q in range(2):
        xr, xi = points_of(in_ref, there, q)
        leave(q, back, hr * xr - hi * xi, hr * xi + hi * xr)
        gr, gi = points_of(in_ref, there, 2 + q)
        leave(2 + q, adjoint, hr * gr + hi * gi, hr * gi - hi * gr)
        real = real + (xr * gr + xi * gi)
        imag = imag + (xr * gi - xi * gr)
    blocks_of(taps_ref, adjoint, real, imag)
    for copy in leaving:
        copy.wait()


def middle_blocks(spectra):
    operands = (spectra,) + tuple(jnp.asarray(t) for t in (THERE, BACK, ADJOINT))
    return pl.pallas_call(
        middle_kernel,
        out_shape=(
            jax.ShapeDtypeStruct((BLOCKS, BACK_ROWS, SIDE), jnp.float32),
            jax.ShapeDtypeStruct((BLOCKS * 16, SIDE), jnp.float32),
        ),
        in_specs=[pl.BlockSpec(memory_space=pltpu.VMEM)] * 4,
        out_specs=(pl.BlockSpec(memory_space=pl.ANY), pl.BlockSpec(memory_space=pltpu.VMEM)),
        scratch_shapes=[pltpu.VMEM((4, BLOCKS, 16, SIDE), jnp.float32), pltpu.SemaphoreType.DMA((4,))],
        compiler_params=pltpu.CompilerParams(vmem_limit_bytes=VMEM_LIMIT),
        name="middle_blocks",
    )(*operands)


def close(in_ref, inner_ref, outer_ref, twist_ref, rows, places):
    cosine, sine = twist_ref[0], twist_ref[1]
    inner = inner_ref[...]
    columns = []
    for p in range(len(places)):
        both = jnp.concatenate(
            [in_ref[:, 16 * p + 8 * h : 16 * p + 8 * h + 8, :].reshape(2 * SIDE, SIDE) for h in range(2)], axis=1
        )
        turned = dot_three(both, inner)
        real, imag = turned[:, :SIDE], turned[:, SIDE:]
        columns.append(jnp.concatenate([real * cosine - imag * sine, imag * cosine + real * sine], axis=0))
    closed = dot_three(outer_ref[...], jnp.concatenate(columns, axis=1))
    for p, pair in enumerate(places):
        for half, place in enumerate(pair):
            rows[place * SIDE : (place + 1) * SIDE, :] = closed[
                half * SIDE : (half + 1) * SIDE, p * SIDE : (p + 1) * SIDE
            ]


def taps_kernel(in_ref, inner_ref, outer_ref, twist_ref, f_ref, rows):
    close(in_ref, inner_ref, outer_ref, twist_ref, rows, ((0, 1),))
    for a in range(SIDE):
        f_ref[:, a * SIDE : (a + 1) * SIDE] = rows[pl.ds(a, 2, stride=SIDE), :]


def inverse_kernel(in_ref, seq_ref, cot_ref, skip_ref, inner_ref, outer_ref, twist_ref, y_ref, g_ref, rows):
    close(in_ref, inner_ref, outer_ref, twist_ref, rows, PAIRS[:4])
    skip = jnp.broadcast_to(skip_ref[...], (4, SIDE))
    for a in range(SIDE):
        lanes = slice(a * SIDE, (a + 1) * SIDE)
        y_ref[:, lanes] = rows[pl.ds(a, 4, stride=SIDE), :] + skip * seq_ref[:, lanes]
        g_ref[:, lanes] = rows[pl.ds(4 * SIDE + a, 4, stride=SIDE), :] + skip * cot_ref[:, lanes]


def taps_blocks(spectra):
    operands = (spectra,) + tuple(jnp.asarray(t) for t in INVERSE_TABLES)
    return call(taps_kernel, "taps_blocks", (2, BLOCK), operands, [pltpu.VMEM((2 * SIDE, SIDE), jnp.float32)])


def inverse_blocks(spectra, sequence, cotangent, skip_gain):
    operands = (spectra, sequence, cotangent, skip_gain[:, None]) + tuple(jnp.asarray(t) for t in INVERSE_TABLES)
    scratch = [pltpu.VMEM((8 * SIDE, SIDE), jnp.float32)]
    return call(inverse_kernel, "inverse_blocks", ((4, BLOCK), (4, BLOCK)), operands, scratch)


def exchange(blocks):
    cut = blocks.reshape(BLOCKS, -1, SIDE)
    return lax.all_to_all(cut, "ctx", split_axis=0, concat_axis=0, tiled=True)


def flip_chan(values, flip):
    return lax.ppermute(values, "chan", [(i, i ^ flip) for i in range(CHAN)])


def sum_over_chan(values):
    for flip in (1, 3, 4):
        values = values + flip_chan(values, flip)
    return values


def body(sequence, filter_taps, skip_gain, cotangent):
    spectra = exchange(forward_blocks(sequence, cotangent, filter_taps)).reshape(BLOCKS * OUT_ROWS, SIDE)
    back, taps = middle_blocks(spectra)
    taps = exchange(taps)
    taps, back = lax.optimization_barrier((taps, back))
    taps_grad = sum_over_chan(taps_blocks(taps))
    convolved, seq_grad = inverse_blocks(exchange(back), sequence, cotangent, skip_gain)
    return convolved, seq_grad, taps_grad


def solution(mesh):
    return jax.shard_map(
        body,
        mesh=mesh,
        in_specs=(P("chan", "ctx"), P(None, "ctx"), P("chan"), P("chan", "ctx")),
        out_specs=(P("chan", "ctx"), P("chan", "ctx"), P(None, "ctx")),
        check_vma=False,
    )
```

```python
import numpy as np
import jax
import jax.numpy as jnp
from jax import lax
from jax.experimental import pallas as pl
from jax.experimental.pallas import tpu as pltpu
from jax.sharding import PartitionSpec as P

SIDE = 128
HALF = SIDE // 2
BLOCK = SIDE * SIDE
BLOCKS = 32
CHAN = 8
OWNERS = BLOCKS * CHAN
POINTS = 2 * BLOCKS
SIGNALS = 8
THERE_ROWS = 9
BACK_ROWS = 10
VMEM_LIMIT = 40 * 1024 * 1024


def make_tables():
    digit = np.arange(SIDE)
    turn = 2.0 * np.pi
    single = np.float32
    angle = turn * ((digit[:, None] + 0.25) * digit[None, :] / SIDE)
    cosine, sine = np.cos(angle), np.sin(angle)
    forward_outer = np.concatenate([cosine, -sine], axis=0)
    factor = (BLOCKS * BLOCK) ** (-0.5) / BLOCK
    inverse_outer = factor * np.concatenate([cosine.T, -sine.T], axis=1)
    angle = turn * ((digit[:, None] * digit[None, :]) % SIDE / SIDE)
    cosine, sine = np.cos(angle), np.sin(angle)
    order = np.arange(2 * SIDE).reshape(2, 2, HALF).transpose(1, 0, 2).reshape(-1)
    forward_inner = np.block([[cosine, -sine], [sine, cosine]])[:, order]
    inverse_inner = np.block([[cosine, sine], [-sine, cosine]])[order, :]
    angle = turn * ((digit[:, None] + 0.25) * digit[None, :] / BLOCK)
    twist = np.stack([np.cos(angle), np.sin(angle)])
    return (
        np.stack([forward_outer, forward_inner[:, :SIDE], forward_inner[:, SIDE:]]).astype(single),
        tuple(t.astype(single) for t in (inverse_inner, inverse_outer, twist)),
    )


def make_block_tables():
    block = np.arange(BLOCKS)
    point = np.arange(POINTS)
    angle = 2.0 * np.pi * ((point[:, None] * block[None, :]) % POINTS) / POINTS
    cosine, sine = np.cos(angle), np.sin(angle)
    tables = [np.block([[cosine, sine], [-sine, cosine]])]
    step = np.exp(-2j * np.pi * point / POINTS)
    for spill in (1.0 + 1j * step, 1.0 - 1j * np.conj(step)):
        back = np.exp(1j * angle.T) * spill[None, :] / POINTS
        tables.append(np.block([[back.real, -back.imag], [back.imag, back.real]]))
    return tuple(t.astype(np.float32) for t in tables)


FORWARD_TABLES, INVERSE_TABLES = make_tables()
BLOCK_TABLES = make_block_tables()


def split(values):
    high = values.astype(jnp.bfloat16)
    return high, (values - high.astype(jnp.float32)).astype(jnp.bfloat16)


def dot(left, right):
    return jnp.dot(left, right, preferred_element_type=jnp.float32)


def dot_three(left, right):
    (lh, ll), (rh, rl) = split(left), split(right)
    return dot(lh, rh) + (dot(lh, rl) + dot(ll, rh))


def dot_wide(left, right):
    (lh, ll), (rh, rl) = split(left), split(right)
    return dot(jnp.concatenate([lh, lh, ll], axis=1), jnp.concatenate([rh, rl, rh], axis=0))


def stacked(table):
    high, low = split(table)
    return jnp.concatenate(
        [jnp.concatenate([high, high], axis=1), jnp.concatenate([low, jnp.zeros_like(low)], axis=1)], axis=0
    )


def dot_stacked(left, right):
    both = dot(left, jnp.concatenate(split(right), axis=0))
    half = both.shape[0] // 2
    return both[:half] + both[half:]


def call(kernel, name, out_shape, operands, scratch=()):
    many = isinstance(out_shape[0], tuple)
    shapes = tuple(jax.ShapeDtypeStruct(s, jnp.float32) for s in (out_shape if many else (out_shape,)))
    outs = (pl.BlockSpec(memory_space=pltpu.VMEM),) * len(shapes)
    return pl.pallas_call(
        kernel,
        out_shape=shapes if many else shapes[0],
        in_specs=[pl.BlockSpec(memory_space=pltpu.VMEM)] * len(operands),
        out_specs=outs if many else outs[0],
        scratch_shapes=list(scratch),
        compiler_params=pltpu.CompilerParams(vmem_limit_bytes=VMEM_LIMIT),
        name=name,
    )(*operands)


def twist_kernel(twist_ref):
    c = lax.broadcasted_iota(jnp.int32, (SIDE, SIDE), 0).astype(jnp.float32)
    b = lax.broadcasted_iota(jnp.int32, (SIDE, SIDE), 1).astype(jnp.float32)
    angle = (c + 0.25) * b * (2.0 * np.pi / BLOCK)
    twist_ref[0] = jnp.cos(angle)
    twist_ref[1] = jnp.sin(angle)


def twist_table():
    return pl.pallas_call(
        twist_kernel,
        out_shape=jax.ShapeDtypeStruct((2, SIDE, SIDE), jnp.float32),
        out_specs=pl.BlockSpec(memory_space=pltpu.VMEM),
        compiler_params=pltpu.CompilerParams(vmem_limit_bytes=4 * 1024 * 1024),
        cost_estimate=pl.CostEstimate(flops=4_000_000_000, bytes_accessed=8_000_000, transcendentals=32768),
        name="twist_table",
    )()


def forward_kernel(seq_ref, cot_ref, taps_ref, tables_ref, twist_ref, out_ref, rows):
    for first, count, source in ((0, 4, seq_ref), (4, 4, cot_ref), (SIGNALS, 2, taps_ref)):
        for a in range(SIDE):
            rows[pl.ds(first * SIDE + a, count, stride=SIDE), :] = source[:, a * SIDE : (a + 1) * SIDE]

    def row(index):
        return rows[index * SIDE : (index + 1) * SIDE, :]

    mine = jnp.where(lax.axis_index("chan") % 2 == 0, row(SIGNALS), row(SIGNALS + 1))
    opened = dot_wide(tables_ref[0], jnp.concatenate([row(i) for i in range(SIGNALS)] + [mine], axis=1))
    cosine, sine = twist_ref[0], twist_ref[1]
    inner = jnp.concatenate([tables_ref[1], tables_ref[2]], axis=1)
    for group in ((0, 1), (2, 3), (4, 5), (6, 7), (8,)):
        twisted = []
        for i in group:
            real = opened[:SIDE, i * SIDE : (i + 1) * SIDE]
            imag = opened[SIDE:, i * SIDE : (i + 1) * SIDE]
            twisted.append(jnp.concatenate([real * cosine + imag * sine, imag * cosine - real * sine], axis=1))
        spectra = dot_three(jnp.concatenate(twisted, axis=0), inner)
        for place, i in enumerate(group):
            for half in range(2):
                out_ref[pl.ds(THERE_ROWS * half + i, SIDE, stride=2 * THERE_ROWS), :] = spectra[
                    place * SIDE : (place + 1) * SIDE, half * SIDE : (half + 1) * SIDE
                ]


def forward_blocks(sequence, cotangent, taps):
    operands = (sequence, cotangent, taps, jnp.asarray(FORWARD_TABLES), twist_table())
    scratch = [pltpu.VMEM((10 * SIDE, SIDE), jnp.float32)]
    return call(forward_kernel, "forward_blocks", (OWNERS * THERE_ROWS, SIDE), operands, scratch)


def middle_kernel(in_ref, there_ref, back_ref, adjoint_ref, out_ref):
    there, back, adjoint = there_ref[...], stacked(back_ref[...]), stacked(adjoint_ref[...])
    low = lax.broadcasted_iota(jnp.int32, (BLOCKS, SIDE), 1) < HALF

    def turn(values):
        return pltpu.roll(values, HALF, 1)

    def arrived(chan, row):
        return in_ref[pl.ds(chan * THERE_ROWS + row, BLOCKS, stride=CHAN * THERE_ROWS), :]

    def leave(chan, row, values):
        out_ref[pl.ds(chan * BACK_ROWS + row, BLOCKS, stride=CHAN * BACK_ROWS), :] = values

    def points_of(first_chan, second_chan, rows):
        reals, imags = [], []
        for r in rows:
            first, second = arrived(first_chan, r), arrived(second_chan, r)
            reals.append(jnp.where(low, first, turn(second)))
            imags.append(jnp.where(low, turn(first), second))
        sides = [jnp.concatenate(reals, axis=1), jnp.concatenate(imags, axis=1)]
        points = dot_wide(there, jnp.concatenate(sides, axis=0))
        return points[:POINTS], points[POINTS:]

    def blocks_of(table, real, imag):
        blocks = dot_stacked(table, jnp.concatenate([real, imag], axis=0))
        return blocks[:BLOCKS], blocks[BLOCKS:]

    filters = [points_of(f, f, (SIGNALS,)) for f in range(2)]
    hr, hi = (jnp.concatenate([filters[f][part] for f in (0, 0, 1, 1)], axis=1) for part in range(2))
    wide = 4 * SIDE
    real = imag = 0.0
    for first in range(0, CHAN, 2):
        pr, pi = points_of(first, first + 1, range(SIGNALS))
        xr, xi, gr, gi = pr[:, :wide], pi[:, :wide], pr[:, wide:], pi[:, wide:]
        real = real + (xr * gr + xi * gi)
        imag = imag + (xr * gi - xi * gr)
        for row, (br, bi) in (
            (0, blocks_of(back, hr * xr - hi * xi, hr * xi + hi * xr)),
            (4, blocks_of(adjoint, hr * gr + hi * gi, hr * gi - hi * gr)),
        ):
            for r in range(4):
                cr, ci = br[:, r * SIDE : (r + 1) * SIDE], bi[:, r * SIDE : (r + 1) * SIDE]
                leave(first, row + r, jnp.where(low, cr, turn(ci)))
                leave(first + 1, row + r, jnp.where(low, turn(cr), ci))

    def over_channels(values):
        sums = [values[:, f * 2 * SIDE : f * 2 * SIDE + SIDE] + values[:, f * 2 * SIDE + SIDE : (f + 1) * 2 * SIDE] for f in range(2)]
        return jnp.concatenate([s + turn(s) for s in sums], axis=1)

    br, bi = blocks_of(adjoint, over_channels(real), over_channels(imag))
    for f in range(2):
        tap = jnp.where(low, br[:, f * SIDE : (f + 1) * SIDE], bi[:, f * SIDE : (f + 1) * SIDE])
        for chan in range(CHAN):
            leave(chan, SIGNALS + f, tap)


def middle_blocks(spectra):
    operands = (spectra,) + tuple(jnp.asarray(t) for t in BLOCK_TABLES)
    return call(middle_kernel, "middle_blocks", (OWNERS * BACK_ROWS, SIDE), operands)


def inverse_kernel(in_ref, seq_ref, cot_ref, skip_ref, inner_ref, outer_ref, twist_ref, y_ref, g_ref, f_ref, rows):
    cosine, sine = twist_ref[0], twist_ref[1]
    inner, outer = inner_ref[...], outer_ref[...]
    for group in ((0, 1), (2, 3), (4, 5), (6, 7), (8, 9)):
        both = jnp.concatenate(
            [
                jnp.concatenate(
                    [in_ref[pl.ds(BACK_ROWS * half + i, SIDE, stride=2 * BACK_ROWS), :] for half in range(2)], axis=1
                )
                for i in group
            ],
            axis=0,
        )
        turned = dot_three(both, inner)
        columns = []
        for place in range(2):
            real = turned[place * SIDE : (place + 1) * SIDE, :SIDE]
            imag = turned[place * SIDE : (place + 1) * SIDE, SIDE:]
            columns.append(jnp.concatenate([real * cosine - imag * sine, imag * cosine + real * sine], axis=0))
        closed = dot_three(outer, jnp.concatenate(columns, axis=1))
        for place, i in enumerate(group):
            rows[i * SIDE : (i + 1) * SIDE, :] = closed[:, place * SIDE : (place + 1) * SIDE]
    skip = jnp.broadcast_to(skip_ref[...], (4, SIDE))
    for a in range(SIDE):
        lanes = slice(a * SIDE, (a + 1) * SIDE)
        y_ref[:, lanes] = rows[pl.ds(a, 4, stride=SIDE), :] + skip * seq_ref[:, lanes]
        g_ref[:, lanes] = rows[pl.ds(4 * SIDE + a, 4, stride=SIDE), :] + skip * cot_ref[:, lanes]
        f_ref[:, lanes] = rows[pl.ds(8 * SIDE + a, 2, stride=SIDE), :]


def inverse_blocks(spectra, sequence, cotangent, skip_gain):
    operands = (spectra, sequence, cotangent, skip_gain[:, None]) + tuple(jnp.asarray(t) for t in INVERSE_TABLES)
    scratch = [pltpu.VMEM((10 * SIDE, SIDE), jnp.float32)]
    return call(inverse_kernel, "inverse_blocks", ((4, BLOCK), (4, BLOCK), (2, BLOCK)), operands, scratch)


def exchange(rows, tall):
    cut = rows.reshape(OWNERS, -1, tall, SIDE)
    return lax.all_to_all(cut, ("ctx", "chan"), split_axis=0, concat_axis=0, tiled=True).reshape(rows.shape)


def body(sequence, filter_taps, skip_gain, cotangent):
    spectra = exchange(forward_blocks(sequence, cotangent, filter_taps), 1)
    products = exchange(middle_blocks(spectra), 2)
    return inverse_blocks(products, sequence, cotangent, skip_gain)


def solution(mesh):
    return jax.shard_map(
        body,
        mesh=mesh,
        in_specs=(P("chan", "ctx"), P(None, "ctx"), P("chan"), P("chan", "ctx")),
        out_specs=(P("chan", "ctx"), P("chan", "ctx"), P(None, "ctx")),
        check_vma=False,
    )
```

```python
import numpy as np
import jax
import jax.numpy as jnp
from jax import lax
from jax.experimental import pallas as pl
from jax.experimental.pallas import tpu as pltpu
from jax.sharding import PartitionSpec as P

SIDE = 128
HALF = SIDE // 2
BLOCK = SIDE * SIDE
BLOCKS = 32
CHAN = 8
OWNERS = BLOCKS * CHAN
POINTS = 2 * BLOCKS
SIGNALS = 8
THERE_ROWS = 9
BACK_ROWS = 10
VMEM_LIMIT = 40 * 1024 * 1024


def make_tables():
    digit = np.arange(SIDE)
    turn = 2.0 * np.pi
    single = np.float32
    angle = turn * ((digit[:, None] + 0.25) * digit[None, :] / SIDE)
    cosine, sine = np.cos(angle), np.sin(angle)
    forward_outer = np.concatenate([cosine, -sine], axis=0)
    factor = (BLOCKS * BLOCK) ** (-0.5) / BLOCK
    inverse_outer = factor * np.concatenate([cosine.T, -sine.T], axis=1)
    angle = turn * ((digit[:, None] * digit[None, :]) % SIDE / SIDE)
    cosine, sine = np.cos(angle), np.sin(angle)
    order = np.arange(2 * SIDE).reshape(2, 2, HALF).transpose(1, 0, 2).reshape(-1)
    forward_inner = np.block([[cosine, -sine], [sine, cosine]])[:, order]
    inverse_inner = np.block([[cosine, sine], [-sine, cosine]])[order, :]
    angle = turn * ((digit[:, None] + 0.25) * digit[None, :] / BLOCK)
    twist = np.stack([np.cos(angle), np.sin(angle)])
    return (
        np.stack([forward_outer, forward_inner[:, :SIDE], forward_inner[:, SIDE:]]).astype(single),
        tuple(t.astype(single) for t in (inverse_inner, inverse_outer, twist)),
    )


def make_block_tables():
    block = np.arange(BLOCKS)
    point = np.arange(POINTS)
    angle = 2.0 * np.pi * ((point[:, None] * block[None, :]) % POINTS) / POINTS
    cosine, sine = np.cos(angle), np.sin(angle)
    tables = [np.block([[cosine, sine], [-sine, cosine]])]
    step = np.exp(-2j * np.pi * point / POINTS)
    for spill in (1.0 + 1j * step, 1.0 - 1j * np.conj(step)):
        back = np.exp(1j * angle.T) * spill[None, :] / POINTS
        tables.append(np.block([[back.real, -back.imag], [back.imag, back.real]]))
    return tuple(t.astype(np.float32) for t in tables)


FORWARD_TABLES, INVERSE_TABLES = make_tables()
BLOCK_TABLES = make_block_tables()


def split(values):
    high = values.astype(jnp.bfloat16)
    return high, (values - high.astype(jnp.float32)).astype(jnp.bfloat16)


def dot(left, right):
    return jnp.dot(left, right, preferred_element_type=jnp.float32)


def dot_three(left, right):
    (lh, ll), (rh, rl) = split(left), split(right)
    return dot(lh, rh) + (dot(lh, rl) + dot(ll, rh))


def dot_wide(left, right):
    (lh, ll), (rh, rl) = split(left), split(right)
    return dot(jnp.concatenate([lh, lh, ll], axis=1), jnp.concatenate([rh, rl, rh], axis=0))


def call(kernel, name, out_shape, operands, scratch=()):
    many = isinstance(out_shape[0], tuple)
    shapes = tuple(jax.ShapeDtypeStruct(s, jnp.float32) for s in (out_shape if many else (out_shape,)))
    outs = (pl.BlockSpec(memory_space=pltpu.VMEM),) * len(shapes)
    return pl.pallas_call(
        kernel,
        out_shape=shapes if many else shapes[0],
        in_specs=[pl.BlockSpec(memory_space=pltpu.VMEM)] * len(operands),
        out_specs=outs if many else outs[0],
        scratch_shapes=list(scratch),
        compiler_params=pltpu.CompilerParams(vmem_limit_bytes=VMEM_LIMIT),
        name=name,
    )(*operands)


def opening_kernel(skip_ref, twist_ref, gain_ref, gains, sem):
    arriving = pltpu.make_async_copy(skip_ref, gains, sem)
    arriving.start()
    c = lax.broadcasted_iota(jnp.int32, (SIDE, SIDE), 0).astype(jnp.float32)
    b = lax.broadcasted_iota(jnp.int32, (SIDE, SIDE), 1).astype(jnp.float32)
    angle = (c + 0.25) * b * (2.0 * np.pi / BLOCK)
    twist_ref[0] = jnp.cos(angle)
    twist_ref[1] = jnp.sin(angle)
    arriving.wait()
    channel = lax.broadcasted_iota(jnp.int32, (4, SIDE), 0)
    gain = jnp.full((4, SIDE), gains[0], jnp.float32)
    for i in range(1, 4):
        gain = jnp.where(channel == i, gains[i], gain)
    gain_ref[...] = gain


def opening(skip_gain):
    return pl.pallas_call(
        opening_kernel,
        out_shape=(
            jax.ShapeDtypeStruct((2, SIDE, SIDE), jnp.float32),
            jax.ShapeDtypeStruct((4, SIDE), jnp.float32),
        ),
        in_specs=[pl.BlockSpec(memory_space=pl.ANY)],
        out_specs=(pl.BlockSpec(memory_space=pltpu.VMEM),) * 2,
        scratch_shapes=[pltpu.SMEM((4,), jnp.float32), pltpu.SemaphoreType.DMA],
        compiler_params=pltpu.CompilerParams(vmem_limit_bytes=4 * 1024 * 1024),
        cost_estimate=pl.CostEstimate(flops=4_000_000_000, bytes_accessed=8_000_000, transcendentals=32768),
        name="opening",
    )(skip_gain)


def forward_kernel(seq_ref, cot_ref, taps_ref, tables_ref, twist_ref, out_ref, rows):
    for first, count, source in ((0, 4, seq_ref), (4, 4, cot_ref), (SIGNALS, 2, taps_ref)):
        for a in range(SIDE):
            rows[pl.ds(first * SIDE + a, count, stride=SIDE), :] = source[:, a * SIDE : (a + 1) * SIDE]

    def row(index):
        return rows[index * SIDE : (index + 1) * SIDE, :]

    mine = jnp.where(lax.axis_index("chan") % 2 == 0, row(SIGNALS), row(SIGNALS + 1))
    opened = dot_wide(tables_ref[0], jnp.concatenate([row(i) for i in range(SIGNALS)] + [mine], axis=1))
    cosine, sine = twist_ref[0], twist_ref[1]
    inner = jnp.concatenate([tables_ref[1], tables_ref[2]], axis=1)
    for group in ((0, 1), (2, 3), (4, 5), (6, 7), (8,)):
        twisted = []
        for i in group:
            real = opened[:SIDE, i * SIDE : (i + 1) * SIDE]
            imag = opened[SIDE:, i * SIDE : (i + 1) * SIDE]
            twisted.append(jnp.concatenate([real * cosine + imag * sine, imag * cosine - real * sine], axis=1))
        spectra = dot_three(jnp.concatenate(twisted, axis=0), inner)
        for place, i in enumerate(group):
            for half in range(2):
                out_ref[pl.ds(THERE_ROWS * half + i, SIDE, stride=2 * THERE_ROWS), :] = spectra[
                    place * SIDE : (place + 1) * SIDE, half * SIDE : (half + 1) * SIDE
                ]


def forward_blocks(sequence, cotangent, taps, twist):
    operands = (sequence, cotangent, taps, jnp.asarray(FORWARD_TABLES), twist)
    scratch = [pltpu.VMEM((10 * SIDE, SIDE), jnp.float32)]
    return call(forward_kernel, "forward_blocks", (OWNERS * THERE_ROWS, SIDE), operands, scratch)


def middle_kernel(in_ref, there_ref, back_ref, adjoint_ref, out_ref):
    there, back, adjoint = there_ref[...], back_ref[...], adjoint_ref[...]
    low = lax.broadcasted_iota(jnp.int32, (BLOCKS, SIDE), 1) < HALF

    def turn(values):
        return pltpu.roll(values, HALF, 1)

    def arrived(chan, row):
        return in_ref[pl.ds(chan * THERE_ROWS + row, BLOCKS, stride=CHAN * THERE_ROWS), :]

    def leave(chan, row, values):
        out_ref[pl.ds(chan * BACK_ROWS + row, BLOCKS, stride=CHAN * BACK_ROWS), :] = values

    def points_of(first_chan, second_chan, rows):
        reals, imags = [], []
        for r in rows:
            first, second = arrived(first_chan, r), arrived(second_chan, r)
            reals.append(jnp.where(low, first, turn(second)))
            imags.append(jnp.where(low, turn(first), second))
        sides = [jnp.concatenate(reals, axis=1), jnp.concatenate(imags, axis=1)]
        points = dot_wide(there, jnp.concatenate(sides, axis=0))
        return points[:POINTS], points[POINTS:]

    def blocks_of(table, real, imag):
        blocks = dot_three(table, jnp.concatenate([real, imag], axis=0))
        return blocks[:BLOCKS], blocks[BLOCKS:]

    filters = [points_of(f, f, (SIGNALS,)) for f in range(2)]
    hr, hi = (jnp.concatenate([filters[f][part] for f in (0, 0, 1, 1)], axis=1) for part in range(2))
    wide = 4 * SIDE
    real = imag = 0.0
    for first in range(0, CHAN, 2):
        pr, pi = points_of(first, first + 1, range(SIGNALS))
        xr, xi, gr, gi = pr[:, :wide], pi[:, :wide], pr[:, wide:], pi[:, wide:]
        real = real + (xr * gr + xi * gi)
        imag = imag + (xr * gi - xi * gr)
        for row, (br, bi) in (
            (0, blocks_of(back, hr * xr - hi * xi, hr * xi + hi * xr)),
            (4, blocks_of(adjoint, hr * gr + hi * gi, hr * gi - hi * gr)),
        ):
            for r in range(4):
                cr, ci = br[:, r * SIDE : (r + 1) * SIDE], bi[:, r * SIDE : (r + 1) * SIDE]
                leave(first, row + r, jnp.where(low, cr, turn(ci)))
                leave(first + 1, row + r, jnp.where(low, turn(cr), ci))

    def over_channels(values):
        sums = [values[:, f * 2 * SIDE : f * 2 * SIDE + SIDE] + values[:, f * 2 * SIDE + SIDE : (f + 1) * 2 * SIDE] for f in range(2)]
        return jnp.concatenate([s + turn(s) for s in sums], axis=1)

    br, bi = blocks_of(adjoint, over_channels(real), over_channels(imag))
    for f in range(2):
        tap = jnp.where(low, br[:, f * SIDE : (f + 1) * SIDE], bi[:, f * SIDE : (f + 1) * SIDE])
        for chan in range(CHAN):
            leave(chan, SIGNALS + f, tap)


def middle_blocks(spectra):
    operands = (spectra,) + tuple(jnp.asarray(t) for t in BLOCK_TABLES)
    return call(middle_kernel, "middle_blocks", (OWNERS * BACK_ROWS, SIDE), operands)


def inverse_kernel(in_ref, seq_ref, cot_ref, gain_ref, inner_ref, outer_ref, twist_ref, y_ref, g_ref, f_ref, rows):
    cosine, sine = twist_ref[0], twist_ref[1]
    inner, outer = inner_ref[...], outer_ref[...]
    gain = gain_ref[...]

    columns = []
    for i in range(10):
        both = [in_ref[pl.ds(BACK_ROWS * half + i, SIDE, stride=2 * BACK_ROWS), :] for half in range(2)]
        turned = dot_three(jnp.concatenate(both, axis=1), inner)
        real, imag = turned[:, :SIDE], turned[:, SIDE:]
        column = jnp.concatenate([real * cosine - imag * sine, imag * cosine + real * sine], axis=0)
        columns.append(column)
    closed = dot_three(outer, jnp.concatenate(columns, axis=1))
    for i in range(10):
        rows[i * SIDE : (i + 1) * SIDE, :] = closed[:, i * SIDE : (i + 1) * SIDE]
    for a in range(SIDE):
        lanes = slice(a * SIDE, (a + 1) * SIDE)
        y_ref[:, lanes] = rows[pl.ds(a, 4, stride=SIDE), :] + gain * seq_ref[:, lanes]
        g_ref[:, lanes] = rows[pl.ds(4 * SIDE + a, 4, stride=SIDE), :] + gain * cot_ref[:, lanes]
        f_ref[:, lanes] = rows[pl.ds(8 * SIDE + a, 2, stride=SIDE), :]


def inverse_blocks(spectra, sequence, cotangent, gain):
    operands = (spectra, sequence, cotangent, gain) + tuple(jnp.asarray(t) for t in INVERSE_TABLES)
    scratch = [pltpu.VMEM((10 * SIDE, SIDE), jnp.float32)]
    return call(inverse_kernel, "inverse_blocks", ((4, BLOCK), (4, BLOCK), (2, BLOCK)), operands, scratch)


def exchange(rows, tall):
    cut = rows.reshape(OWNERS, -1, tall, SIDE)
    return lax.all_to_all(cut, ("ctx", "chan"), split_axis=0, concat_axis=0, tiled=True).reshape(rows.shape)


def body(sequence, filter_taps, skip_gain, cotangent):
    twist, gain = opening(skip_gain)
    spectra = exchange(forward_blocks(sequence, cotangent, filter_taps, twist), 1)
    products = exchange(middle_blocks(spectra), 2)
    return inverse_blocks(products, sequence, cotangent, gain)


def solution(mesh):
    return jax.shard_map(
        body,
        mesh=mesh,
        in_specs=(P("chan", "ctx"), P(None, "ctx"), P("chan"), P("chan", "ctx")),
        out_specs=(P("chan", "ctx"), P("chan", "ctx"), P(None, "ctx")),
        check_vma=False,
    )
```

```python
import numpy as np
import jax
import jax.numpy as jnp
from jax import lax
from jax.experimental import pallas as pl
from jax.experimental.pallas import tpu as pltpu
from jax.sharding import PartitionSpec as P

SIDE = 128
HALF = SIDE // 2
BLOCK = SIDE * SIDE
BLOCKS = 32
CHAN = 8
OWNERS = BLOCKS * CHAN
POINTS = 2 * BLOCKS
SIGNALS = 8
THERE_ROWS = 9
BACK_ROWS = 10
VMEM_LIMIT = 40 * 1024 * 1024


def make_tables():
    digit = np.arange(SIDE)
    turn = 2.0 * np.pi
    single = np.float32
    angle = turn * ((digit[:, None] + 0.25) * digit[None, :] / SIDE)
    cosine, sine = np.cos(angle), np.sin(angle)
    forward_outer = np.concatenate([cosine, -sine], axis=0)
    factor = (BLOCKS * BLOCK) ** (-0.5) / BLOCK
    inverse_outer = factor * np.concatenate([cosine.T, -sine.T], axis=1)
    angle = turn * ((digit[:, None] * digit[None, :]) % SIDE / SIDE)
    cosine, sine = np.cos(angle), np.sin(angle)
    order = np.arange(2 * SIDE).reshape(2, 2, HALF).transpose(1, 0, 2).reshape(-1)
    forward_inner = np.block([[cosine, -sine], [sine, cosine]])[:, order]
    inverse_inner = np.block([[cosine, sine], [-sine, cosine]])[order, :]
    angle = turn * ((digit[:, None] + 0.25) * digit[None, :] / BLOCK)
    twist = np.stack([np.cos(angle), np.sin(angle)])
    return (
        np.stack([forward_outer, forward_inner[:, :SIDE], forward_inner[:, SIDE:]]).astype(single),
        tuple(t.astype(single) for t in (inverse_inner, inverse_outer, twist)),
    )


def make_block_tables():
    block = np.arange(BLOCKS)
    point = np.arange(POINTS)
    angle = 2.0 * np.pi * ((point[:, None] * block[None, :]) % POINTS) / POINTS
    cosine, sine = np.cos(angle), np.sin(angle)
    tables = [np.block([[cosine, sine], [-sine, cosine]])]
    step = np.exp(-2j * np.pi * point / POINTS)
    for spill in (1.0 + 1j * step, 1.0 - 1j * np.conj(step)):
        back = np.exp(1j * angle.T) * spill[None, :] / POINTS
        tables.append(np.block([[back.real, -back.imag], [back.imag, back.real]]))
    return tuple(t.astype(np.float32) for t in tables)


FORWARD_TABLES, INVERSE_TABLES = make_tables()
BLOCK_TABLES = make_block_tables()


def split(values):
    high = values.astype(jnp.bfloat16)
    return high, (values - high.astype(jnp.float32)).astype(jnp.bfloat16)


def dot(left, right):
    return jnp.dot(left, right, preferred_element_type=jnp.float32)


def dot_three(left, right):
    (lh, ll), (rh, rl) = split(left), split(right)
    return dot(lh, rh) + (dot(lh, rl) + dot(ll, rh))


def dot_wide(left, right):
    (lh, ll), (rh, rl) = split(left), split(right)
    return dot(jnp.concatenate([lh, lh, ll], axis=1), jnp.concatenate([rh, rl, rh], axis=0))


def call(kernel, name, out_shape, operands, scratch=()):
    many = isinstance(out_shape[0], tuple)
    shapes = tuple(jax.ShapeDtypeStruct(s, jnp.float32) for s in (out_shape if many else (out_shape,)))
    outs = (pl.BlockSpec(memory_space=pltpu.VMEM),) * len(shapes)
    return pl.pallas_call(
        kernel,
        out_shape=shapes if many else shapes[0],
        in_specs=[pl.BlockSpec(memory_space=pltpu.VMEM)] * len(operands),
        out_specs=outs if many else outs[0],
        scratch_shapes=list(scratch),
        compiler_params=pltpu.CompilerParams(vmem_limit_bytes=VMEM_LIMIT),
        name=name,
    )(*operands)


def twist_kernel(twist_ref):
    c = lax.broadcasted_iota(jnp.int32, (SIDE, SIDE), 0).astype(jnp.float32)
    b = lax.broadcasted_iota(jnp.int32, (SIDE, SIDE), 1).astype(jnp.float32)
    angle = (c + 0.25) * b * (2.0 * np.pi / BLOCK)
    twist_ref[0] = jnp.cos(angle)
    twist_ref[1] = jnp.sin(angle)


def twist_table():
    return pl.pallas_call(
        twist_kernel,
        out_shape=jax.ShapeDtypeStruct((2, SIDE, SIDE), jnp.float32),
        out_specs=pl.BlockSpec(memory_space=pltpu.VMEM),
        compiler_params=pltpu.CompilerParams(vmem_limit_bytes=4 * 1024 * 1024),
        cost_estimate=pl.CostEstimate(flops=4_000_000_000, bytes_accessed=8_000_000, transcendentals=32768),
        name="twist_table",
    )()


def forward_kernel(seq_ref, cot_ref, taps_ref, tables_ref, twist_ref, out_ref, rows):
    for first, count, source in ((0, 4, seq_ref), (4, 4, cot_ref), (SIGNALS, 2, taps_ref)):
        for a in range(SIDE):
            rows[pl.ds(first * SIDE + a, count, stride=SIDE), :] = source[:, a * SIDE : (a + 1) * SIDE]

    def row(index):
        return rows[index * SIDE : (index + 1) * SIDE, :]

    mine = jnp.where(lax.axis_index("chan") % 2 == 0, row(SIGNALS), row(SIGNALS + 1))
    opened = dot_wide(tables_ref[0], jnp.concatenate([row(i) for i in range(SIGNALS)] + [mine], axis=1))
    cosine, sine = twist_ref[0], twist_ref[1]
    inner = jnp.concatenate([tables_ref[1], tables_ref[2]], axis=1)
    for group in ((0, 1), (2, 3), (4, 5), (6, 7), (8,)):
        twisted = []
        for i in group:
            real = opened[:SIDE, i * SIDE : (i + 1) * SIDE]
            imag = opened[SIDE:, i * SIDE : (i + 1) * SIDE]
            twisted.append(jnp.concatenate([real * cosine + imag * sine, imag * cosine - real * sine], axis=1))
        spectra = dot_three(jnp.concatenate(twisted, axis=0), inner)
        for place, i in enumerate(group):
            for half in range(2):
                out_ref[pl.ds(THERE_ROWS * half + i, SIDE, stride=2 * THERE_ROWS), :] = spectra[
                    place * SIDE : (place + 1) * SIDE, half * SIDE : (half + 1) * SIDE
                ]


def forward_blocks(sequence, cotangent, taps):
    operands = (sequence, cotangent, taps, jnp.asarray(FORWARD_TABLES), twist_table())
    scratch = [pltpu.VMEM((10 * SIDE, SIDE), jnp.float32)]
    return call(forward_kernel, "forward_blocks", (OWNERS * THERE_ROWS, SIDE), operands, scratch)


def middle_kernel(in_ref, there_ref, back_ref, adjoint_ref, out_ref):
    there, back, adjoint = there_ref[...], back_ref[...], adjoint_ref[...]
    low = lax.broadcasted_iota(jnp.int32, (BLOCKS, SIDE), 1) < HALF

    def turn(values):
        return pltpu.roll(values, HALF, 1)

    def arrived(chan, row):
        return in_ref[pl.ds(chan * THERE_ROWS + row, BLOCKS, stride=CHAN * THERE_ROWS), :]

    def leave(chan, row, values):
        out_ref[pl.ds(chan * BACK_ROWS + row, BLOCKS, stride=CHAN * BACK_ROWS), :] = values

    def points_of(first_chan, second_chan, rows):
        reals, imags = [], []
        for r in rows:
            first, second = arrived(first_chan, r), arrived(second_chan, r)
            reals.append(jnp.where(low, first, turn(second)))
            imags.append(jnp.where(low, turn(first), second))
        sides = [jnp.concatenate(reals, axis=1), jnp.concatenate(imags, axis=1)]
        points = dot_wide(there, jnp.concatenate(sides, axis=0))
        return points[:POINTS], points[POINTS:]

    def blocks_of(table, real, imag):
        blocks = dot_three(table, jnp.concatenate([real, imag], axis=0))
        return blocks[:BLOCKS], blocks[BLOCKS:]

    filters = [points_of(f, f, (SIGNALS,)) for f in range(2)]
    hr, hi = (jnp.concatenate([filters[f][part] for f in (0, 0, 1, 1)], axis=1) for part in range(2))
    wide = 4 * SIDE
    real = imag = 0.0
    for first in range(0, CHAN, 2):
        pr, pi = points_of(first, first + 1, range(SIGNALS))
        xr, xi, gr, gi = pr[:, :wide], pi[:, :wide], pr[:, wide:], pi[:, wide:]
        real = real + (xr * gr + xi * gi)
        imag = imag + (xr * gi - xi * gr)
        for row, (br, bi) in (
            (0, blocks_of(back, hr * xr - hi * xi, hr * xi + hi * xr)),
            (4, blocks_of(adjoint, hr * gr + hi * gi, hr * gi - hi * gr)),
        ):
            for r in range(4):
                cr, ci = br[:, r * SIDE : (r + 1) * SIDE], bi[:, r * SIDE : (r + 1) * SIDE]
                leave(first, row + r, jnp.where(low, cr, turn(ci)))
                leave(first + 1, row + r, jnp.where(low, turn(cr), ci))

    def over_channels(values):
        sums = [values[:, f * 2 * SIDE : f * 2 * SIDE + SIDE] + values[:, f * 2 * SIDE + SIDE : (f + 1) * 2 * SIDE] for f in range(2)]
        return jnp.concatenate([s + turn(s) for s in sums], axis=1)

    br, bi = blocks_of(adjoint, over_channels(real), over_channels(imag))
    for f in range(2):
        tap = jnp.where(low, br[:, f * SIDE : (f + 1) * SIDE], bi[:, f * SIDE : (f + 1) * SIDE])
        for chan in range(CHAN):
            leave(chan, SIGNALS + f, tap)


def middle_blocks(spectra):
    operands = (spectra,) + tuple(jnp.asarray(t) for t in BLOCK_TABLES)
    return call(middle_kernel, "middle_blocks", (OWNERS * BACK_ROWS, SIDE), operands)


def inverse_kernel(in_ref, seq_ref, cot_ref, skip_ref, inner_ref, outer_ref, twist_ref, y_ref, g_ref, f_ref, rows):
    cosine, sine = twist_ref[0], twist_ref[1]
    inner, outer = inner_ref[...], outer_ref[...]
    gain = jnp.concatenate([jnp.broadcast_to(skip_ref[:, i : i + 1], (1, SIDE)) for i in range(4)], axis=0)

    columns = []
    for i in range(10):
        both = [in_ref[pl.ds(BACK_ROWS * half + i, SIDE, stride=2 * BACK_ROWS), :] for half in range(2)]
        turned = dot_three(jnp.concatenate(both, axis=1), inner)
        real, imag = turned[:, :SIDE], turned[:, SIDE:]
        column = jnp.concatenate([real * cosine - imag * sine, imag * cosine + real * sine], axis=0)
        columns.append(column)
    closed = dot_three(outer, jnp.concatenate(columns, axis=1))
    for i in range(10):
        rows[i * SIDE : (i + 1) * SIDE, :] = closed[:, i * SIDE : (i + 1) * SIDE]
    for a in range(SIDE):
        lanes = slice(a * SIDE, (a + 1) * SIDE)
        y_ref[:, lanes] = rows[pl.ds(a, 4, stride=SIDE), :] + gain * seq_ref[:, lanes]
        g_ref[:, lanes] = rows[pl.ds(4 * SIDE + a, 4, stride=SIDE), :] + gain * cot_ref[:, lanes]
        f_ref[:, lanes] = rows[pl.ds(8 * SIDE + a, 2, stride=SIDE), :]


def inverse_blocks(spectra, sequence, cotangent, skip_gain):
    operands = (spectra, sequence, cotangent, skip_gain[None, :]) + tuple(jnp.asarray(t) for t in INVERSE_TABLES)
    scratch = [pltpu.VMEM((10 * SIDE, SIDE), jnp.float32)]
    return call(inverse_kernel, "inverse_blocks", ((4, BLOCK), (4, BLOCK), (2, BLOCK)), operands, scratch)


def exchange(rows, tall):
    cut = rows.reshape(OWNERS, -1, tall, SIDE)
    return lax.all_to_all(cut, ("ctx", "chan"), split_axis=0, concat_axis=0, tiled=True).reshape(rows.shape)


def body(sequence, filter_taps, skip_gain, cotangent):
    spectra = exchange(forward_blocks(sequence, cotangent, filter_taps), 1)
    products = exchange(middle_blocks(spectra), 2)
    return inverse_blocks(products, sequence, cotangent, skip_gain)


def solution(mesh):
    return jax.shard_map(
        body,
        mesh=mesh,
        in_specs=(P("chan", "ctx"), P(None, "ctx"), P("chan"), P("chan", "ctx")),
        out_specs=(P("chan", "ctx"), P("chan", "ctx"), P(None, "ctx")),
        check_vma=False,
    )
```

```python
import numpy as np
import jax
import jax.numpy as jnp
from jax import lax
from jax.experimental import pallas as pl
from jax.experimental.pallas import tpu as pltpu
from jax.sharding import PartitionSpec as P

SIDE = 128
HALF = SIDE // 2
BLOCK = SIDE * SIDE
BLOCKS = 32
CHAN = 8
OWNERS = BLOCKS * CHAN
POINTS = 2 * BLOCKS
SIGNALS = 8
THERE_ROWS = 9
BACK_ROWS = 10
VMEM_LIMIT = 40 * 1024 * 1024


def make_tables():
    digit = np.arange(SIDE)
    turn = 2.0 * np.pi
    single = np.float32
    angle = turn * ((digit[:, None] + 0.25) * digit[None, :] / SIDE)
    cosine, sine = np.cos(angle), np.sin(angle)
    forward_outer = np.concatenate([cosine, -sine], axis=0)
    factor = (BLOCKS * BLOCK) ** (-0.5) / BLOCK
    inverse_outer = factor * np.concatenate([cosine.T, -sine.T], axis=1)
    angle = turn * ((digit[:, None] * digit[None, :]) % SIDE / SIDE)
    cosine, sine = np.cos(angle), np.sin(angle)
    order = np.arange(2 * SIDE).reshape(2, 2, HALF).transpose(1, 0, 2).reshape(-1)
    forward_inner = np.block([[cosine, -sine], [sine, cosine]])[:, order]
    inverse_inner = np.block([[cosine, sine], [-sine, cosine]])[order, :]
    angle = turn * ((digit[:, None] + 0.25) * digit[None, :] / BLOCK)
    twist = np.stack([np.cos(angle), np.sin(angle)])
    return (
        np.stack([forward_outer, forward_inner[:, :SIDE], forward_inner[:, SIDE:]]).astype(single),
        tuple(t.astype(single) for t in (inverse_inner, inverse_outer, twist)),
    )


def make_block_tables():
    block = np.arange(BLOCKS)
    point = np.arange(POINTS)
    angle = 2.0 * np.pi * ((point[:, None] * block[None, :]) % POINTS) / POINTS
    cosine, sine = np.cos(angle), np.sin(angle)
    tables = [np.block([[cosine, sine], [-sine, cosine]])]
    step = np.exp(-2j * np.pi * point / POINTS)
    for spill in (1.0 + 1j * step, 1.0 - 1j * np.conj(step)):
        back = np.exp(1j * angle.T) * spill[None, :] / POINTS
        tables.append(np.block([[back.real, -back.imag], [back.imag, back.real]]))
    return tuple(t.astype(np.float32) for t in tables)


FORWARD_TABLES, INVERSE_TABLES = make_tables()
BLOCK_TABLES = make_block_tables()


def split(values):
    high = values.astype(jnp.bfloat16)
    return high, (values - high.astype(jnp.float32)).astype(jnp.bfloat16)


def dot(left, right):
    return jnp.dot(left, right, preferred_element_type=jnp.float32)


def dot_three(left, right):
    (lh, ll), (rh, rl) = split(left), split(right)
    return dot(lh, rh) + (dot(lh, rl) + dot(ll, rh))


def dot_wide(left, right):
    (lh, ll), (rh, rl) = split(left), split(right)
    return dot(jnp.concatenate([lh, lh, ll], axis=1), jnp.concatenate([rh, rl, rh], axis=0))


def call(kernel, name, out_shape, operands, scratch=()):
    many = isinstance(out_shape[0], tuple)
    shapes = tuple(jax.ShapeDtypeStruct(s, jnp.float32) for s in (out_shape if many else (out_shape,)))
    outs = (pl.BlockSpec(memory_space=pltpu.VMEM),) * len(shapes)
    return pl.pallas_call(
        kernel,
        out_shape=shapes if many else shapes[0],
        in_specs=[pl.BlockSpec(memory_space=pltpu.VMEM)] * len(operands),
        out_specs=outs if many else outs[0],
        scratch_shapes=list(scratch),
        compiler_params=pltpu.CompilerParams(vmem_limit_bytes=VMEM_LIMIT),
        name=name,
    )(*operands)


def twist_kernel(twist_ref):
    c = lax.broadcasted_iota(jnp.int32, (SIDE, SIDE), 0).astype(jnp.float32)
    b = lax.broadcasted_iota(jnp.int32, (SIDE, SIDE), 1).astype(jnp.float32)
    angle = (c + 0.25) * b * (2.0 * np.pi / BLOCK)
    twist_ref[0] = jnp.cos(angle)
    twist_ref[1] = jnp.sin(angle)


def twist_table():
    return pl.pallas_call(
        twist_kernel,
        out_shape=jax.ShapeDtypeStruct((2, SIDE, SIDE), jnp.float32),
        out_specs=pl.BlockSpec(memory_space=pltpu.VMEM),
        compiler_params=pltpu.CompilerParams(vmem_limit_bytes=4 * 1024 * 1024),
        cost_estimate=pl.CostEstimate(flops=4_000_000_000, bytes_accessed=8_000_000, transcendentals=32768),
        name="twist_table",
    )()


def forward_kernel(seq_ref, cot_ref, taps_ref, tables_ref, twist_ref, out_ref, rows):
    for first, count, source in ((0, 4, seq_ref), (4, 4, cot_ref), (SIGNALS, 2, taps_ref)):
        for a in range(SIDE):
            rows[pl.ds(first * SIDE + a, count, stride=SIDE), :] = source[:, a * SIDE : (a + 1) * SIDE]

    def row(index):
        return rows[index * SIDE : (index + 1) * SIDE, :]

    mine = jnp.where(lax.axis_index("chan") % 2 == 0, row(SIGNALS), row(SIGNALS + 1))
    opened = dot_wide(tables_ref[0], jnp.concatenate([row(i) for i in range(SIGNALS)] + [mine], axis=1))
    cosine, sine = twist_ref[0], twist_ref[1]
    inner = jnp.concatenate([tables_ref[1], tables_ref[2]], axis=1)
    for group in ((0, 1), (2, 3), (4, 5), (6, 7), (8,)):
        twisted = []
        for i in group:
            real = opened[:SIDE, i * SIDE : (i + 1) * SIDE]
            imag = opened[SIDE:, i * SIDE : (i + 1) * SIDE]
            twisted.append(jnp.concatenate([real * cosine + imag * sine, imag * cosine - real * sine], axis=1))
        spectra = dot_three(jnp.concatenate(twisted, axis=0), inner)
        for place, i in enumerate(group):
            for half in range(2):
                out_ref[pl.ds(THERE_ROWS * half + i, SIDE, stride=2 * THERE_ROWS), :] = spectra[
                    place * SIDE : (place + 1) * SIDE, half * SIDE : (half + 1) * SIDE
                ]


def forward_blocks(sequence, cotangent, taps):
    operands = (sequence, cotangent, taps, jnp.asarray(FORWARD_TABLES), twist_table())
    scratch = [pltpu.VMEM((10 * SIDE, SIDE), jnp.float32)]
    return call(forward_kernel, "forward_blocks", (OWNERS * THERE_ROWS, SIDE), operands, scratch)


def middle_kernel(in_ref, there_ref, back_ref, adjoint_ref, out_ref):
    there, back, adjoint = there_ref[...], back_ref[...], adjoint_ref[...]
    low = lax.broadcasted_iota(jnp.int32, (BLOCKS, SIDE), 1) < HALF

    def turn(values):
        return pltpu.roll(values, HALF, 1)

    def arrived(chan, row):
        return in_ref[pl.ds(chan * THERE_ROWS + row, BLOCKS, stride=CHAN * THERE_ROWS), :]

    def leave(chan, row, values):
        out_ref[pl.ds(chan * BACK_ROWS + row, BLOCKS, stride=CHAN * BACK_ROWS), :] = values

    def points_of(first_chan, second_chan, rows):
        reals, imags = [], []
        for r in rows:
            first, second = arrived(first_chan, r), arrived(second_chan, r)
            reals.append(jnp.where(low, first, turn(second)))
            imags.append(jnp.where(low, turn(first), second))
        sides = [jnp.concatenate(reals, axis=1), jnp.concatenate(imags, axis=1)]
        points = dot_wide(there, jnp.concatenate(sides, axis=0))
        return points[:POINTS], points[POINTS:]

    def blocks_of(table, real, imag):
        blocks = dot_three(table, jnp.concatenate([real, imag], axis=0))
        return blocks[:BLOCKS], blocks[BLOCKS:]

    filters = [points_of(f, f, (SIGNALS,)) for f in range(2)]
    hr, hi = (jnp.concatenate([filters[f][part] for f in (0, 0, 1, 1)], axis=1) for part in range(2))
    wide = 4 * SIDE
    real = imag = 0.0
    for first in range(0, CHAN, 2):
        pr, pi = points_of(first, first + 1, range(SIGNALS))
        xr, xi, gr, gi = pr[:, :wide], pi[:, :wide], pr[:, wide:], pi[:, wide:]
        real = real + (xr * gr + xi * gi)
        imag = imag + (xr * gi - xi * gr)
        for row, (br, bi) in (
            (0, blocks_of(back, hr * xr - hi * xi, hr * xi + hi * xr)),
            (4, blocks_of(adjoint, hr * gr + hi * gi, hr * gi - hi * gr)),
        ):
            for r in range(4):
                cr, ci = br[:, r * SIDE : (r + 1) * SIDE], bi[:, r * SIDE : (r + 1) * SIDE]
                leave(first, row + r, jnp.where(low, cr, turn(ci)))
                leave(first + 1, row + r, jnp.where(low, turn(cr), ci))

    def over_channels(values):
        sums = [values[:, f * 2 * SIDE : f * 2 * SIDE + SIDE] + values[:, f * 2 * SIDE + SIDE : (f + 1) * 2 * SIDE] for f in range(2)]
        return jnp.concatenate([s + turn(s) for s in sums], axis=1)

    br, bi = blocks_of(adjoint, over_channels(real), over_channels(imag))
    for f in range(2):
        tap = jnp.where(low, br[:, f * SIDE : (f + 1) * SIDE], bi[:, f * SIDE : (f + 1) * SIDE])
        for chan in range(CHAN):
            leave(chan, SIGNALS + f, tap)


def middle_blocks(spectra):
    operands = (spectra,) + tuple(jnp.asarray(t) for t in BLOCK_TABLES)
    return call(middle_kernel, "middle_blocks", (OWNERS * BACK_ROWS, SIDE), operands)


def inverse_kernel(in_ref, seq_ref, cot_ref, skip_ref, inner_ref, outer_ref, twist_ref, y_ref, g_ref, f_ref, rows):
    cosine, sine = twist_ref[0], twist_ref[1]
    inner, outer = inner_ref[...], outer_ref[...]
    gain = jnp.concatenate([jnp.broadcast_to(skip_ref[:, i : i + 1], (1, SIDE)) for i in range(4)], axis=0)

    columns = []
    for i in range(10):
        both = [in_ref[pl.ds(BACK_ROWS * half + i, SIDE, stride=2 * BACK_ROWS), :] for half in range(2)]
        turned = dot_three(jnp.concatenate(both, axis=1), inner)
        real, imag = turned[:, :SIDE], turned[:, SIDE:]
        column = jnp.concatenate([real * cosine - imag * sine, imag * cosine + real * sine], axis=0)
        columns.append(column)
    closed = dot_wide(outer, jnp.concatenate(columns, axis=1))
    for i in range(10):
        rows[i * SIDE : (i + 1) * SIDE, :] = closed[:, i * SIDE : (i + 1) * SIDE]
    for a in range(SIDE):
        lanes = slice(a * SIDE, (a + 1) * SIDE)
        y_ref[:, lanes] = rows[pl.ds(a, 4, stride=SIDE), :] + gain * seq_ref[:, lanes]
        g_ref[:, lanes] = rows[pl.ds(4 * SIDE + a, 4, stride=SIDE), :] + gain * cot_ref[:, lanes]
        f_ref[:, lanes] = rows[pl.ds(8 * SIDE + a, 2, stride=SIDE), :]


def inverse_blocks(spectra, sequence, cotangent, skip_gain):
    operands = (spectra, sequence, cotangent, skip_gain[None, :]) + tuple(jnp.asarray(t) for t in INVERSE_TABLES)
    scratch = [pltpu.VMEM((10 * SIDE, SIDE), jnp.float32)]
    return call(inverse_kernel, "inverse_blocks", ((4, BLOCK), (4, BLOCK), (2, BLOCK)), operands, scratch)


def exchange(rows, tall):
    cut = rows.reshape(OWNERS, -1, tall, SIDE)
    return lax.all_to_all(cut, ("ctx", "chan"), split_axis=0, concat_axis=0, tiled=True).reshape(rows.shape)


def body(sequence, filter_taps, skip_gain, cotangent):
    spectra = exchange(forward_blocks(sequence, cotangent, filter_taps), 1)
    products = exchange(middle_blocks(spectra), 2)
    return inverse_blocks(products, sequence, cotangent, skip_gain)


def solution(mesh):
    return jax.shard_map(
        body,
        mesh=mesh,
        in_specs=(P("chan", "ctx"), P(None, "ctx"), P("chan"), P("chan", "ctx")),
        out_specs=(P("chan", "ctx"), P("chan", "ctx"), P(None, "ctx")),
        check_vma=False,
    )
```

```python
import numpy as np
import jax
import jax.numpy as jnp
from jax import lax
from jax.experimental import pallas as pl
from jax.experimental.pallas import tpu as pltpu
from jax.sharding import PartitionSpec as P

SIDE = 128
BLOCK = SIDE * SIDE
BLOCKS = 32
CHAN = 8
OWNERS = BLOCKS * CHAN
POINTS = 2 * BLOCKS
THERE_ROWS = 9
BACK_ROWS = 10
VMEM_LIMIT = 40 * 1024 * 1024


def make_tables():
    digit = np.arange(SIDE)
    turn = 2.0 * np.pi
    single = np.float32
    angle = turn * ((digit[:, None] + 0.25) * digit[None, :] / SIDE)
    cosine, sine = np.cos(angle), np.sin(angle)
    forward_outer = np.concatenate([cosine, -sine], axis=0)
    factor = (BLOCKS * BLOCK) ** (-0.5) / BLOCK
    inverse_outer = factor * np.concatenate([cosine.T, -sine.T], axis=1)
    angle = turn * ((digit[:, None] * digit[None, :]) % SIDE / SIDE)
    cosine, sine = np.cos(angle), np.sin(angle)
    forward_inner = np.block([[cosine, -sine], [sine, cosine]])
    inverse_inner = np.block([[cosine, sine], [-sine, cosine]])
    angle = turn * ((digit[:, None] + 0.25) * digit[None, :] / BLOCK)
    twist = np.stack([np.cos(angle), np.sin(angle)])
    return (
        np.stack([forward_outer, forward_inner[:, :SIDE], forward_inner[:, SIDE:]]).astype(single),
        tuple(t.astype(single) for t in (inverse_inner, inverse_outer, twist)),
    )


def make_block_tables():
    block = np.arange(BLOCKS)
    point = np.arange(POINTS)
    angle = 2.0 * np.pi * ((point[:, None] * block[None, :]) % POINTS) / POINTS
    cosine, sine = np.cos(angle), np.sin(angle)
    tables = [np.block([[cosine, sine], [-sine, cosine]])]
    step = np.exp(-2j * np.pi * point / POINTS)
    for spill in (1.0 + 1j * step, 1.0 - 1j * np.conj(step)):
        back = np.exp(1j * angle.T) * spill[None, :] / POINTS
        tables.append(np.block([[back.real, -back.imag], [back.imag, back.real]]))
    return tuple(t.astype(np.float32) for t in tables)


FORWARD_TABLES, INVERSE_TABLES = make_tables()
BLOCK_TABLES = make_block_tables()


def split(values):
    high = values.astype(jnp.bfloat16)
    return high, (values - high.astype(jnp.float32)).astype(jnp.bfloat16)


def dot(left, right):
    return jnp.dot(left, right, preferred_element_type=jnp.float32)


def dot_three(left, right):
    (lh, ll), (rh, rl) = split(left), split(right)
    return dot(lh, rh) + (dot(lh, rl) + dot(ll, rh))


def dot_wide(left, right):
    (lh, ll), (rh, rl) = split(left), split(right)
    return dot(jnp.concatenate([lh, lh, ll], axis=1), jnp.concatenate([rh, rl, rh], axis=0))


def call(kernel, name, out_shape, operands, scratch=()):
    many = isinstance(out_shape[0], tuple)
    shapes = tuple(jax.ShapeDtypeStruct(s, jnp.float32) for s in (out_shape if many else (out_shape,)))
    outs = (pl.BlockSpec(memory_space=pltpu.VMEM),) * len(shapes)
    return pl.pallas_call(
        kernel,
        out_shape=shapes if many else shapes[0],
        in_specs=[pl.BlockSpec(memory_space=pltpu.VMEM)] * len(operands),
        out_specs=outs if many else outs[0],
        scratch_shapes=list(scratch),
        compiler_params=pltpu.CompilerParams(vmem_limit_bytes=VMEM_LIMIT),
        name=name,
    )(*operands)


def twist_kernel(twist_ref):
    c = lax.broadcasted_iota(jnp.int32, (SIDE, SIDE), 0).astype(jnp.float32)
    b = lax.broadcasted_iota(jnp.int32, (SIDE, SIDE), 1).astype(jnp.float32)
    angle = (c + 0.25) * b * (2.0 * np.pi / BLOCK)
    twist_ref[0] = jnp.cos(angle)
    twist_ref[1] = jnp.sin(angle)


def twist_table():
    return pl.pallas_call(
        twist_kernel,
        out_shape=jax.ShapeDtypeStruct((2, SIDE, SIDE), jnp.float32),
        out_specs=pl.BlockSpec(memory_space=pltpu.VMEM),
        compiler_params=pltpu.CompilerParams(vmem_limit_bytes=4 * 1024 * 1024),
        cost_estimate=pl.CostEstimate(flops=4_000_000_000, bytes_accessed=8_000_000, transcendentals=32768),
        name="twist_table",
    )()


def place_of(signal):
    kind, channel = divmod(signal, 4)
    return (channel, 8) if kind == 2 else (channel // 2, 4 * kind + 2 * (channel % 2))


def forward_kernel(seq_ref, cot_ref, taps_ref, tables_ref, twist_ref, out_ref, rows):
    for first, count, source in ((0, 4, seq_ref), (4, 4, cot_ref), (8, 2, taps_ref)):
        for a in range(SIDE):
            rows[pl.ds(first * SIDE + a, count, stride=SIDE), :] = source[:, a * SIDE : (a + 1) * SIDE]

    signals = jnp.concatenate([rows[i * SIDE : (i + 1) * SIDE, :] for i in range(10)], axis=1)
    opened = dot_wide(tables_ref[0], signals)
    cosine, sine = twist_ref[0], twist_ref[1]
    inner = jnp.concatenate([tables_ref[1], tables_ref[2]], axis=1)
    sends_real = lax.axis_index("chan") % 2 == 0

    def leave(filt, row, values):
        out_ref[pl.ds(THERE_ROWS * filt + row, SIDE, stride=2 * THERE_ROWS), :] = values

    for group in ((0, 1), (2, 3), (4, 5), (6, 7), (8, 9)):
        twisted = []
        for i in group:
            real = opened[:SIDE, i * SIDE : (i + 1) * SIDE]
            imag = opened[SIDE:, i * SIDE : (i + 1) * SIDE]
            twisted.append(jnp.concatenate([real * cosine + imag * sine, imag * cosine - real * sine], axis=1))
        spectra = dot_three(jnp.concatenate(twisted, axis=0), inner)
        for place, i in enumerate(group):
            real = spectra[place * SIDE : (place + 1) * SIDE, :SIDE]
            imag = spectra[place * SIDE : (place + 1) * SIDE, SIDE:]
            filt, row = place_of(i)
            if row == 8:
                leave(filt, row, jnp.where(sends_real, real, imag))
            else:
                leave(filt, row, real)
                leave(filt, row + 1, imag)


def forward_blocks(sequence, cotangent, taps):
    operands = (sequence, cotangent, taps, jnp.asarray(FORWARD_TABLES), twist_table())
    scratch = [pltpu.VMEM((10 * SIDE, SIDE), jnp.float32)]
    return call(forward_kernel, "forward_blocks", (OWNERS * THERE_ROWS, SIDE), operands, scratch)


def middle_kernel(in_ref, there_ref, back_ref, adjoint_ref, out_ref):
    there, back, adjoint = there_ref[...], back_ref[...], adjoint_ref[...]

    def points_of(places):
        sides = [
            jnp.concatenate(
                [
                    in_ref[pl.ds(chan * THERE_ROWS + row, BLOCKS, stride=CHAN * THERE_ROWS), :]
                    for chan, row in places(part)
                ],
                axis=1,
            )
            for part in range(2)
        ]
        points = dot_wide(there, jnp.concatenate(sides, axis=0))
        return points[:POINTS], points[POINTS:]

    def leave(table, places, real, imag):
        blocks = dot_wide(table, jnp.concatenate([real, imag], axis=0))
        for part in range(2):
            lines = slice(part * BLOCKS, (part + 1) * BLOCKS)
            for n, (chan, row) in places:
                out_ref[pl.ds(chan * BACK_ROWS + row + part, BLOCKS, stride=CHAN * BACK_ROWS), :] = blocks[
                    lines, n * SIDE : (n + 1) * SIDE
                ]

    def over_channels(values):
        return sum(values[:, n * SIDE : (n + 1) * SIDE] for n in range(len(first_kind)))

    first_kind = [(chan, row) for chan in range(CHAN) for row in (0, 2)]
    second_kind = [(chan, row + 4) for chan, row in first_kind]
    hr, hi = points_of(lambda part: [(part, 8)])
    hr, hi = (jnp.concatenate([part] * len(first_kind), axis=1) for part in (hr, hi))
    pr, pi = points_of(lambda part: [(chan, row + part) for chan, row in first_kind + second_kind])
    wide = len(first_kind) * SIDE
    xr, xi, gr, gi = pr[:, :wide], pi[:, :wide], pr[:, wide:], pi[:, wide:]
    leave(back, list(enumerate(first_kind)), hr * xr - hi * xi, hr * xi + hi * xr)
    leave(adjoint, list(enumerate(second_kind)), hr * gr + hi * gi, hr * gi - hi * gr)
    leave(
        adjoint,
        [(0, (chan, 8)) for chan in range(CHAN)],
        over_channels(xr * gr + xi * gi),
        over_channels(xr * gi - xi * gr),
    )


def middle_blocks(spectra):
    operands = (spectra,) + tuple(jnp.asarray(t) for t in BLOCK_TABLES)
    return call(middle_kernel, "middle_blocks", (OWNERS * BACK_ROWS, SIDE), operands)


def inverse_kernel(in_ref, seq_ref, cot_ref, skip_ref, inner_ref, outer_ref, twist_ref, y_ref, g_ref, f_ref, rows):
    cosine, sine = twist_ref[0], twist_ref[1]
    inner, outer = inner_ref[...], outer_ref[...]
    gain = jnp.concatenate([jnp.broadcast_to(skip_ref[:, i : i + 1], (1, SIDE)) for i in range(4)], axis=0)

    columns = []
    for i in range(10):
        filt, row = place_of(i)
        both = [in_ref[pl.ds(BACK_ROWS * filt + row + p, SIDE, stride=2 * BACK_ROWS), :] for p in range(2)]
        turned = dot_three(jnp.concatenate(both, axis=1), inner)
        real, imag = turned[:, :SIDE], turned[:, SIDE:]
        column = jnp.concatenate([real * cosine - imag * sine, imag * cosine + real * sine], axis=0)
        columns.append(column)
    closed = dot_wide(outer, jnp.concatenate(columns, axis=1))
    for i in range(10):
        rows[i * SIDE : (i + 1) * SIDE, :] = closed[:, i * SIDE : (i + 1) * SIDE]
    for a in range(SIDE):
        lanes = slice(a * SIDE, (a + 1) * SIDE)
        y_ref[:, lanes] = rows[pl.ds(a, 4, stride=SIDE), :] + gain * seq_ref[:, lanes]
        g_ref[:, lanes] = rows[pl.ds(4 * SIDE + a, 4, stride=SIDE), :] + gain * cot_ref[:, lanes]
        f_ref[:, lanes] = rows[pl.ds(8 * SIDE + a, 2, stride=SIDE), :]


def inverse_blocks(spectra, sequence, cotangent, skip_gain):
    operands = (spectra, sequence, cotangent, skip_gain[None, :]) + tuple(jnp.asarray(t) for t in INVERSE_TABLES)
    scratch = [pltpu.VMEM((10 * SIDE, SIDE), jnp.float32)]
    return call(inverse_kernel, "inverse_blocks", ((4, BLOCK), (4, BLOCK), (2, BLOCK)), operands, scratch)


def exchange(rows, tall):
    cut = rows.reshape(OWNERS, -1, tall, SIDE)
    return lax.all_to_all(cut, ("ctx", "chan"), split_axis=0, concat_axis=0, tiled=True).reshape(rows.shape)


def body(sequence, filter_taps, skip_gain, cotangent):
    spectra = exchange(forward_blocks(sequence, cotangent, filter_taps), 1)
    products = exchange(middle_blocks(spectra), 2)
    return inverse_blocks(products, sequence, cotangent, skip_gain)


def solution(mesh):
    return jax.shard_map(
        body,
        mesh=mesh,
        in_specs=(P("chan", "ctx"), P(None, "ctx"), P("chan"), P("chan", "ctx")),
        out_specs=(P("chan", "ctx"), P("chan", "ctx"), P(None, "ctx")),
        check_vma=False,
    )
```

```python
import numpy as np
import jax
import jax.numpy as jnp
from jax import lax
from jax.experimental import pallas as pl
from jax.experimental.pallas import tpu as pltpu
from jax.sharding import PartitionSpec as P

SIDE = 128
BLOCK = SIDE * SIDE
BLOCKS = 32
CHAN = 8
OWNERS = BLOCKS * CHAN
POINTS = 2 * BLOCKS
THERE_ROWS = 9
BACK_ROWS = 10
VMEM_LIMIT = 40 * 1024 * 1024


def make_tables():
    digit = np.arange(SIDE)
    turn = 2.0 * np.pi
    single = np.float32
    angle = turn * ((digit[:, None] + 0.25) * digit[None, :] / SIDE)
    cosine, sine = np.cos(angle), np.sin(angle)
    forward_outer = np.concatenate([cosine, -sine], axis=0)
    factor = (BLOCKS * BLOCK) ** (-0.5) / BLOCK
    inverse_outer = factor * np.concatenate([cosine.T, -sine.T], axis=1)
    angle = turn * ((digit[:, None] * digit[None, :]) % SIDE / SIDE)
    cosine, sine = np.cos(angle), np.sin(angle)
    forward_inner = np.block([[cosine, -sine], [sine, cosine]])
    inverse_inner = np.block([[cosine, sine], [-sine, cosine]])
    angle = turn * ((digit[:, None] + 0.25) * digit[None, :] / BLOCK)
    twist = np.stack([np.cos(angle), np.sin(angle)])
    return (
        np.stack([forward_outer, forward_inner[:, :SIDE], forward_inner[:, SIDE:]]).astype(single),
        tuple(t.astype(single) for t in (inverse_inner, inverse_outer, twist)),
    )


def make_block_tables():
    block = np.arange(BLOCKS)
    point = np.arange(POINTS)
    angle = 2.0 * np.pi * ((point[:, None] * block[None, :]) % POINTS) / POINTS
    cosine, sine = np.cos(angle), np.sin(angle)
    tables = [np.block([[cosine, sine], [-sine, cosine]])]
    step = np.exp(-2j * np.pi * point / POINTS)
    for spill in (1.0 + 1j * step, 1.0 - 1j * np.conj(step)):
        back = np.exp(1j * angle.T) * spill[None, :] / POINTS
        tables.append(np.block([[back.real, -back.imag], [back.imag, back.real]]))
    return tuple(t.astype(np.float32) for t in tables)


FORWARD_TABLES, INVERSE_TABLES = make_tables()
BLOCK_TABLES = make_block_tables()


def split(values):
    high = values.astype(jnp.bfloat16)
    return high, (values - high.astype(jnp.float32)).astype(jnp.bfloat16)


def dot(left, right):
    return jnp.dot(left, right, preferred_element_type=jnp.float32)


def dot_three(left, right):
    (lh, ll), (rh, rl) = split(left), split(right)
    return dot(lh, rh) + (dot(lh, rl) + dot(ll, rh))


def dot_wide(left, right):
    (lh, ll), (rh, rl) = split(left), split(right)
    return dot(jnp.concatenate([lh, lh, ll], axis=1), jnp.concatenate([rh, rl, rh], axis=0))


def call(kernel, name, out_shape, operands, scratch=()):
    many = isinstance(out_shape[0], tuple)
    shapes = tuple(jax.ShapeDtypeStruct(s, jnp.float32) for s in (out_shape if many else (out_shape,)))
    outs = (pl.BlockSpec(memory_space=pltpu.VMEM),) * len(shapes)
    return pl.pallas_call(
        kernel,
        out_shape=shapes if many else shapes[0],
        in_specs=[pl.BlockSpec(memory_space=pltpu.VMEM)] * len(operands),
        out_specs=outs if many else outs[0],
        scratch_shapes=list(scratch),
        compiler_params=pltpu.CompilerParams(vmem_limit_bytes=VMEM_LIMIT),
        name=name,
    )(*operands)


def twist_kernel(twist_ref):
    c = lax.broadcasted_iota(jnp.int32, (SIDE, SIDE), 0).astype(jnp.float32)
    b = lax.broadcasted_iota(jnp.int32, (SIDE, SIDE), 1).astype(jnp.float32)
    angle = (c + 0.25) * b * (2.0 * np.pi / BLOCK)
    twist_ref[0] = jnp.cos(angle)
    twist_ref[1] = jnp.sin(angle)


def twist_table():
    return pl.pallas_call(
        twist_kernel,
        out_shape=jax.ShapeDtypeStruct((2, SIDE, SIDE), jnp.float32),
        out_specs=pl.BlockSpec(memory_space=pltpu.VMEM),
        compiler_params=pltpu.CompilerParams(vmem_limit_bytes=4 * 1024 * 1024),
        cost_estimate=pl.CostEstimate(flops=4_000_000_000, bytes_accessed=8_000_000, transcendentals=32768),
        name="twist_table",
    )()


def place_of(signal):
    kind, channel = divmod(signal, 4)
    return (channel, 8) if kind == 2 else (channel // 2, 4 * kind + 2 * (channel % 2))


def forward_kernel(seq_ref, cot_ref, taps_ref, tables_ref, twist_ref, out_ref):
    signals = jnp.concatenate(
        [
            source[i : i + 1, :].reshape(SIDE, SIDE)
            for count, source in ((4, seq_ref), (4, cot_ref), (2, taps_ref))
            for i in range(count)
        ],
        axis=1,
    )
    opened = dot_wide(tables_ref[0], signals)
    cosine, sine = twist_ref[0], twist_ref[1]
    inner = jnp.concatenate([tables_ref[1], tables_ref[2]], axis=1)
    sends_real = lax.axis_index("chan") % 2 == 0

    def leave(filt, row, values):
        out_ref[pl.ds(THERE_ROWS * filt + row, SIDE, stride=2 * THERE_ROWS), :] = values

    for group in ((0, 1), (2, 3), (4, 5), (6, 7), (8, 9)):
        twisted = []
        for i in group:
            real = opened[:SIDE, i * SIDE : (i + 1) * SIDE]
            imag = opened[SIDE:, i * SIDE : (i + 1) * SIDE]
            twisted.append(jnp.concatenate([real * cosine + imag * sine, imag * cosine - real * sine], axis=1))
        spectra = dot_three(jnp.concatenate(twisted, axis=0), inner)
        for place, i in enumerate(group):
            real = spectra[place * SIDE : (place + 1) * SIDE, :SIDE]
            imag = spectra[place * SIDE : (place + 1) * SIDE, SIDE:]
            filt, row = place_of(i)
            if row == 8:
                leave(filt, row, jnp.where(sends_real, real, imag))
            else:
                leave(filt, row, real)
                leave(filt, row + 1, imag)


def forward_blocks(sequence, cotangent, taps):
    operands = (sequence, cotangent, taps, jnp.asarray(FORWARD_TABLES), twist_table())
    return call(forward_kernel, "forward_blocks", (OWNERS * THERE_ROWS, SIDE), operands)


def middle_kernel(in_ref, there_ref, back_ref, adjoint_ref, out_ref):
    there, back, adjoint = there_ref[...], back_ref[...], adjoint_ref[...]

    def points_of(places):
        sides = [
            jnp.concatenate(
                [
                    in_ref[pl.ds(chan * THERE_ROWS + row, BLOCKS, stride=CHAN * THERE_ROWS), :]
                    for chan, row in places(part)
                ],
                axis=1,
            )
            for part in range(2)
        ]
        points = dot_wide(there, jnp.concatenate(sides, axis=0))
        return points[:POINTS], points[POINTS:]

    def leave(table, places, real, imag):
        blocks = dot_wide(table, jnp.concatenate([real, imag], axis=0))
        for part in range(2):
            lines = slice(part * BLOCKS, (part + 1) * BLOCKS)
            for n, (chan, row) in places:
                out_ref[pl.ds(chan * BACK_ROWS + row + part, BLOCKS, stride=CHAN * BACK_ROWS), :] = blocks[
                    lines, n * SIDE : (n + 1) * SIDE
                ]

    def over_channels(values):
        return sum(values[:, n * SIDE : (n + 1) * SIDE] for n in range(len(first_kind)))

    first_kind = [(chan, row) for chan in range(CHAN) for row in (0, 2)]
    second_kind = [(chan, row + 4) for chan, row in first_kind]
    hr, hi = points_of(lambda part: [(part, 8)])
    hr, hi = (jnp.concatenate([part] * len(first_kind), axis=1) for part in (hr, hi))
    pr, pi = points_of(lambda part: [(chan, row + part) for chan, row in first_kind + second_kind])
    wide = len(first_kind) * SIDE
    xr, xi, gr, gi = pr[:, :wide], pi[:, :wide], pr[:, wide:], pi[:, wide:]
    leave(back, list(enumerate(first_kind)), hr * xr - hi * xi, hr * xi + hi * xr)
    leave(adjoint, list(enumerate(second_kind)), hr * gr + hi * gi, hr * gi - hi * gr)
    leave(
        adjoint,
        [(0, (chan, 8)) for chan in range(CHAN)],
        over_channels(xr * gr + xi * gi),
        over_channels(xr * gi - xi * gr),
    )


def middle_blocks(spectra):
    operands = (spectra,) + tuple(jnp.asarray(t) for t in BLOCK_TABLES)
    return call(middle_kernel, "middle_blocks", (OWNERS * BACK_ROWS, SIDE), operands)


def inverse_kernel(in_ref, seq_ref, cot_ref, skip_ref, inner_ref, outer_ref, twist_ref, y_ref, g_ref, f_ref):
    cosine, sine = twist_ref[0], twist_ref[1]
    inner, outer = inner_ref[...], outer_ref[...]

    columns = []
    for i in range(10):
        filt, row = place_of(i)
        both = [in_ref[pl.ds(BACK_ROWS * filt + row + p, SIDE, stride=2 * BACK_ROWS), :] for p in range(2)]
        turned = dot_three(jnp.concatenate(both, axis=1), inner)
        real, imag = turned[:, :SIDE], turned[:, SIDE:]
        column = jnp.concatenate([real * cosine - imag * sine, imag * cosine + real * sine], axis=0)
        columns.append(column)
    closed = dot_wide(outer, jnp.concatenate(columns, axis=1))

    def line(signal):
        return closed[:, signal * SIDE : (signal + 1) * SIDE].reshape(1, BLOCK)

    for c in range(4):
        gain = skip_ref[:, c : c + 1]
        y_ref[c : c + 1, :] = line(c) + gain * seq_ref[c : c + 1, :]
        g_ref[c : c + 1, :] = line(4 + c) + gain * cot_ref[c : c + 1, :]
    for c in range(2):
        f_ref[c : c + 1, :] = line(8 + c)


def inverse_blocks(spectra, sequence, cotangent, skip_gain):
    operands = (spectra, sequence, cotangent, skip_gain[None, :]) + tuple(jnp.asarray(t) for t in INVERSE_TABLES)
    return call(inverse_kernel, "inverse_blocks", ((4, BLOCK), (4, BLOCK), (2, BLOCK)), operands)


def exchange(rows, tall):
    cut = rows.reshape(OWNERS, -1, tall, SIDE)
    return lax.all_to_all(cut, ("ctx", "chan"), split_axis=0, concat_axis=0, tiled=True).reshape(rows.shape)


def body(sequence, filter_taps, skip_gain, cotangent):
    spectra = exchange(forward_blocks(sequence, cotangent, filter_taps), 1)
    products = exchange(middle_blocks(spectra), 2)
    return inverse_blocks(products, sequence, cotangent, skip_gain)


def solution(mesh):
    return jax.shard_map(
        body,
        mesh=mesh,
        in_specs=(P("chan", "ctx"), P(None, "ctx"), P("chan"), P("chan", "ctx")),
        out_specs=(P("chan", "ctx"), P("chan", "ctx"), P(None, "ctx")),
        check_vma=False,
    )
```

```python
import numpy as np
import jax
import jax.numpy as jnp
from jax import lax
from jax.experimental import pallas as pl
from jax.experimental.pallas import tpu as pltpu
from jax.sharding import PartitionSpec as P

SIDE = 128
BLOCK = SIDE * SIDE
BLOCKS = 32
CHAN = 8
OWNERS = BLOCKS * CHAN
POINTS = 2 * BLOCKS
THERE_ROWS = 9
BACK_ROWS = 10
VMEM_LIMIT = 40 * 1024 * 1024


def make_tables():
    digit = np.arange(SIDE)
    turn = 2.0 * np.pi
    single = np.float32
    angle = turn * ((digit[:, None] + 0.25) * digit[None, :] / SIDE)
    cosine, sine = np.cos(angle), np.sin(angle)
    forward_outer = np.concatenate([cosine, -sine], axis=0)
    factor = (BLOCKS * BLOCK) ** (-0.5) / BLOCK
    inverse_outer = factor * np.concatenate([cosine.T, -sine.T], axis=1)
    angle = turn * ((digit[:, None] * digit[None, :]) % SIDE / SIDE)
    cosine, sine = np.cos(angle), np.sin(angle)
    forward_inner = np.block([[cosine, -sine], [sine, cosine]])
    inverse_inner = np.block([[cosine, sine], [-sine, cosine]])
    angle = turn * ((digit[:, None] + 0.25) * digit[None, :] / BLOCK)
    twist = np.stack([np.cos(angle), np.sin(angle)])
    return (
        np.stack([forward_outer, forward_inner[:, :SIDE]]).astype(single),
        tuple(t.astype(single) for t in (inverse_inner, inverse_outer, twist)),
    )


def make_block_tables():
    block = np.arange(BLOCKS)
    point = np.arange(POINTS)
    angle = 2.0 * np.pi * ((point[:, None] * block[None, :]) % POINTS) / POINTS
    cosine, sine = np.cos(angle), np.sin(angle)
    tables = [np.block([[cosine, sine], [-sine, cosine]])]
    step = np.exp(-2j * np.pi * point / POINTS)
    for spill in (1.0 + 1j * step, 1.0 - 1j * np.conj(step)):
        back = np.exp(1j * angle.T) * spill[None, :] / POINTS
        tables.append(np.block([[back.real, -back.imag], [back.imag, back.real]]))
    return tuple(t.astype(np.float32) for t in tables)


FORWARD_TABLES, INVERSE_TABLES = make_tables()
BLOCK_TABLES = make_block_tables()


def split(values):
    high = values.astype(jnp.bfloat16)
    return high, (values - high.astype(jnp.float32)).astype(jnp.bfloat16)


def dot(left, right):
    return jnp.dot(left, right, preferred_element_type=jnp.float32)


def dot_three(left, right):
    (lh, ll), (rh, rl) = split(left), split(right)
    return dot(lh, rh) + (dot(lh, rl) + dot(ll, rh))


def dot_wide(left, right):
    (lh, ll), (rh, rl) = split(left), split(right)
    return dot(jnp.concatenate([lh, lh, ll], axis=1), jnp.concatenate([rh, rl, rh], axis=0))


def call(kernel, name, out_shape, operands, scratch=()):
    many = isinstance(out_shape[0], tuple)
    shapes = tuple(jax.ShapeDtypeStruct(s, jnp.float32) for s in (out_shape if many else (out_shape,)))
    outs = (pl.BlockSpec(memory_space=pltpu.VMEM),) * len(shapes)
    return pl.pallas_call(
        kernel,
        out_shape=shapes if many else shapes[0],
        in_specs=[pl.BlockSpec(memory_space=pltpu.VMEM)] * len(operands),
        out_specs=outs if many else outs[0],
        scratch_shapes=list(scratch),
        compiler_params=pltpu.CompilerParams(vmem_limit_bytes=VMEM_LIMIT),
        name=name,
    )(*operands)


def twist_kernel(twist_ref):
    c = lax.broadcasted_iota(jnp.int32, (SIDE, SIDE), 0).astype(jnp.float32)
    b = lax.broadcasted_iota(jnp.int32, (SIDE, SIDE), 1).astype(jnp.float32)
    angle = (c + 0.25) * b * (2.0 * np.pi / BLOCK)
    twist_ref[0] = jnp.cos(angle)
    twist_ref[1] = jnp.sin(angle)


def twist_table():
    return pl.pallas_call(
        twist_kernel,
        out_shape=jax.ShapeDtypeStruct((2, SIDE, SIDE), jnp.float32),
        out_specs=pl.BlockSpec(memory_space=pltpu.VMEM),
        compiler_params=pltpu.CompilerParams(vmem_limit_bytes=4 * 1024 * 1024),
        cost_estimate=pl.CostEstimate(flops=4_000_000_000, bytes_accessed=8_000_000, transcendentals=32768),
        name="twist_table",
    )()


def place_of(signal):
    kind, channel = divmod(signal, 4)
    return (channel, 8) if kind == 2 else (channel // 2, 4 * kind + 2 * (channel % 2))


def forward_kernel(seq_ref, cot_ref, taps_ref, tables_ref, twist_ref, out_ref):
    signals = jnp.concatenate(
        [
            source[i : i + 1, :].reshape(SIDE, SIDE)
            for count, source in ((4, seq_ref), (4, cot_ref), (2, taps_ref))
            for i in range(count)
        ],
        axis=1,
    )
    opened = dot_wide(tables_ref[0], signals)
    cosine, sine = twist_ref[0], twist_ref[1]
    across = tables_ref[1]
    inner = jnp.concatenate([across, jnp.concatenate([-across[SIDE:], across[:SIDE]], axis=0)], axis=1)
    sends_real = lax.axis_index("chan") % 2 == 0

    def leave(filt, row, values):
        out_ref[pl.ds(THERE_ROWS * filt + row, SIDE, stride=2 * THERE_ROWS), :] = values

    for group in ((0, 1), (2, 3), (4, 5), (6, 7), (8, 9)):
        twisted = []
        for i in group:
            real = opened[:SIDE, i * SIDE : (i + 1) * SIDE]
            imag = opened[SIDE:, i * SIDE : (i + 1) * SIDE]
            twisted.append(jnp.concatenate([real * cosine + imag * sine, imag * cosine - real * sine], axis=1))
        spectra = dot_three(jnp.concatenate(twisted, axis=0), inner)
        for place, i in enumerate(group):
            real = spectra[place * SIDE : (place + 1) * SIDE, :SIDE]
            imag = spectra[place * SIDE : (place + 1) * SIDE, SIDE:]
            filt, row = place_of(i)
            if row == 8:
                leave(filt, row, jnp.where(sends_real, real, imag))
            else:
                leave(filt, row, real)
                leave(filt, row + 1, imag)


def forward_blocks(sequence, cotangent, taps):
    operands = (sequence, cotangent, taps, jnp.asarray(FORWARD_TABLES), twist_table())
    return call(forward_kernel, "forward_blocks", (OWNERS * THERE_ROWS, SIDE), operands)


def middle_kernel(in_ref, there_ref, back_ref, adjoint_ref, out_ref):
    there, back, adjoint = there_ref[...], back_ref[...], adjoint_ref[...]

    def points_of(places):
        sides = [
            jnp.concatenate(
                [
                    in_ref[pl.ds(chan * THERE_ROWS + row, BLOCKS, stride=CHAN * THERE_ROWS), :]
                    for chan, row in places(part)
                ],
                axis=1,
            )
            for part in range(2)
        ]
        points = dot_wide(there, jnp.concatenate(sides, axis=0))
        return points[:POINTS], points[POINTS:]

    def leave(table, places, real, imag):
        blocks = dot_wide(table, jnp.concatenate([real, imag], axis=0))
        for part in range(2):
            lines = slice(part * BLOCKS, (part + 1) * BLOCKS)
            for n, (chan, row) in places:
                out_ref[pl.ds(chan * BACK_ROWS + row + part, BLOCKS, stride=CHAN * BACK_ROWS), :] = blocks[
                    lines, n * SIDE : (n + 1) * SIDE
                ]

    def over_channels(values):
        return sum(values[:, n * SIDE : (n + 1) * SIDE] for n in range(len(first_kind)))

    first_kind = [(chan, row) for chan in range(CHAN) for row in (0, 2)]
    second_kind = [(chan, row + 4) for chan, row in first_kind]
    hr, hi = points_of(lambda part: [(part, 8)])
    hr, hi = (jnp.concatenate([part] * len(first_kind), axis=1) for part in (hr, hi))
    pr, pi = points_of(lambda part: [(chan, row + part) for chan, row in first_kind + second_kind])
    wide = len(first_kind) * SIDE
    xr, xi, gr, gi = pr[:, :wide], pi[:, :wide], pr[:, wide:], pi[:, wide:]
    leave(back, list(enumerate(first_kind)), hr * xr - hi * xi, hr * xi + hi * xr)
    leave(adjoint, list(enumerate(second_kind)), hr * gr + hi * gi, hr * gi - hi * gr)
    leave(
        adjoint,
        [(0, (chan, 8)) for chan in range(CHAN)],
        over_channels(xr * gr + xi * gi),
        over_channels(xr * gi - xi * gr),
    )


def middle_blocks(spectra):
    operands = (spectra,) + tuple(jnp.asarray(t) for t in BLOCK_TABLES)
    return call(middle_kernel, "middle_blocks", (OWNERS * BACK_ROWS, SIDE), operands)


def inverse_kernel(in_ref, seq_ref, cot_ref, skip_ref, inner_ref, outer_ref, twist_ref, y_ref, g_ref, f_ref):
    cosine, sine = twist_ref[0], twist_ref[1]
    inner, outer = inner_ref[...], outer_ref[...]

    columns = []
    for i in range(10):
        filt, row = place_of(i)
        both = [in_ref[pl.ds(BACK_ROWS * filt + row + p, SIDE, stride=2 * BACK_ROWS), :] for p in range(2)]
        turned = dot_three(jnp.concatenate(both, axis=1), inner)
        real, imag = turned[:, :SIDE], turned[:, SIDE:]
        column = jnp.concatenate([real * cosine - imag * sine, imag * cosine + real * sine], axis=0)
        columns.append(column)
    closed = dot_wide(outer, jnp.concatenate(columns, axis=1))

    def line(signal):
        return closed[:, signal * SIDE : (signal + 1) * SIDE].reshape(1, BLOCK)

    for c in range(4):
        gain = skip_ref[:, c : c + 1]
        y_ref[c : c + 1, :] = line(c) + gain * seq_ref[c : c + 1, :]
        g_ref[c : c + 1, :] = line(4 + c) + gain * cot_ref[c : c + 1, :]
    for c in range(2):
        f_ref[c : c + 1, :] = line(8 + c)


def inverse_blocks(spectra, sequence, cotangent, skip_gain):
    operands = (spectra, sequence, cotangent, skip_gain[None, :]) + tuple(jnp.asarray(t) for t in INVERSE_TABLES)
    return call(inverse_kernel, "inverse_blocks", ((4, BLOCK), (4, BLOCK), (2, BLOCK)), operands)


def exchange(rows, tall):
    cut = rows.reshape(OWNERS, -1, tall, SIDE)
    return lax.all_to_all(cut, ("ctx", "chan"), split_axis=0, concat_axis=0, tiled=True).reshape(rows.shape)


def body(sequence, filter_taps, skip_gain, cotangent):
    spectra = exchange(forward_blocks(sequence, cotangent, filter_taps), 1)
    products = exchange(middle_blocks(spectra), 2)
    return inverse_blocks(products, sequence, cotangent, skip_gain)


def solution(mesh):
    return jax.shard_map(
        body,
        mesh=mesh,
        in_specs=(P("chan", "ctx"), P(None, "ctx"), P("chan"), P("chan", "ctx")),
        out_specs=(P("chan", "ctx"), P("chan", "ctx"), P(None, "ctx")),
        check_vma=False,
    )
```

```python
import numpy as np
import jax
import jax.numpy as jnp
from jax import lax
from jax.experimental import pallas as pl
from jax.experimental.pallas import tpu as pltpu
from jax.sharding import PartitionSpec as P

SIDE = 128
BLOCK = SIDE * SIDE
BLOCKS = 32
CHAN = 8
OWNERS = BLOCKS * CHAN
POINTS = 2 * BLOCKS
THERE_ROWS = 9
BACK_ROWS = 10
VMEM_LIMIT = 40 * 1024 * 1024


def make_tables():
    digit = np.arange(SIDE)
    turn = 2.0 * np.pi
    single = np.float32
    angle = turn * ((digit[:, None] + 0.25) * digit[None, :] / SIDE)
    cosine, sine = np.cos(angle), np.sin(angle)
    forward_outer = np.concatenate([cosine, -sine], axis=0)
    factor = (BLOCKS * BLOCK) ** (-0.5) / BLOCK
    inverse_outer = factor * np.concatenate([cosine.T, -sine.T], axis=1)
    angle = turn * ((digit[:, None] * digit[None, :]) % SIDE / SIDE)
    cosine, sine = np.cos(angle), np.sin(angle)
    forward_inner = np.block([[cosine, -sine], [sine, cosine]])
    inverse_inner = np.block([[cosine, sine], [-sine, cosine]])
    angle = turn * ((digit[:, None] + 0.25) * digit[None, :] / BLOCK)
    twist = np.stack([np.cos(angle), np.sin(angle)])
    return (
        forward_inner[:, :SIDE].astype(single),
        tuple(t.astype(single) for t in (inverse_inner, inverse_outer, twist)),
    )


def make_block_tables():
    block = np.arange(BLOCKS)
    point = np.arange(POINTS)
    angle = 2.0 * np.pi * ((point[:, None] * block[None, :]) % POINTS) / POINTS
    cosine, sine = np.cos(angle), np.sin(angle)
    tables = [np.block([[cosine, sine], [-sine, cosine]])]
    step = np.exp(-2j * np.pi * point / POINTS)
    for spill in (1.0 + 1j * step, 1.0 - 1j * np.conj(step)):
        back = np.exp(1j * angle.T) * spill[None, :] / POINTS
        tables.append(np.block([[back.real, -back.imag], [back.imag, back.real]]))
    return tuple(t.astype(np.float32) for t in tables)


FORWARD_TABLES, INVERSE_TABLES = make_tables()
BLOCK_TABLES = make_block_tables()


def split(values):
    high = values.astype(jnp.bfloat16)
    return high, (values - high.astype(jnp.float32)).astype(jnp.bfloat16)


def dot(left, right):
    return jnp.dot(left, right, preferred_element_type=jnp.float32)


def dot_three(left, right):
    (lh, ll), (rh, rl) = split(left), split(right)
    return dot(lh, rh) + (dot(lh, rl) + dot(ll, rh))


def dot_wide(left, right):
    (lh, ll), (rh, rl) = split(left), split(right)
    return dot(jnp.concatenate([lh, lh, ll], axis=1), jnp.concatenate([rh, rl, rh], axis=0))


def call(kernel, name, out_shape, operands, scratch=()):
    many = isinstance(out_shape[0], tuple)
    shapes = tuple(jax.ShapeDtypeStruct(s, jnp.float32) for s in (out_shape if many else (out_shape,)))
    outs = (pl.BlockSpec(memory_space=pltpu.VMEM),) * len(shapes)
    return pl.pallas_call(
        kernel,
        out_shape=shapes if many else shapes[0],
        in_specs=[pl.BlockSpec(memory_space=pltpu.VMEM)] * len(operands),
        out_specs=outs if many else outs[0],
        scratch_shapes=list(scratch),
        compiler_params=pltpu.CompilerParams(vmem_limit_bytes=VMEM_LIMIT),
        name=name,
    )(*operands)


def twist_kernel(twist_ref):
    c = lax.broadcasted_iota(jnp.int32, (SIDE, SIDE), 0).astype(jnp.float32)
    b = lax.broadcasted_iota(jnp.int32, (SIDE, SIDE), 1).astype(jnp.float32)
    angle = (c + 0.25) * b * (2.0 * np.pi / BLOCK)
    twist_ref[0] = jnp.cos(angle)
    twist_ref[1] = jnp.sin(angle)
    quarter_turns = (4 * lax.broadcasted_iota(jnp.int32, (SIDE, SIDE), 0) + 1) * lax.broadcasted_iota(
        jnp.int32, (SIDE, SIDE), 1
    )
    angle = (quarter_turns & (4 * SIDE - 1)).astype(jnp.float32) * (2.0 * np.pi / (4 * SIDE))
    twist_ref[2] = jnp.cos(angle)
    twist_ref[3] = -jnp.sin(angle)


def twist_table():
    return pl.pallas_call(
        twist_kernel,
        out_shape=jax.ShapeDtypeStruct((4, SIDE, SIDE), jnp.float32),
        out_specs=pl.BlockSpec(memory_space=pltpu.VMEM),
        compiler_params=pltpu.CompilerParams(vmem_limit_bytes=4 * 1024 * 1024),
        cost_estimate=pl.CostEstimate(flops=4_000_000_000, bytes_accessed=8_000_000, transcendentals=32768),
        name="twist_table",
    )()


def place_of(signal):
    kind, channel = divmod(signal, 4)
    return (channel, 8) if kind == 2 else (channel // 2, 4 * kind + 2 * (channel % 2))


def forward_kernel(seq_ref, cot_ref, taps_ref, tables_ref, twist_ref, out_ref):
    signals = jnp.concatenate(
        [
            source[i : i + 1, :].reshape(SIDE, SIDE)
            for count, source in ((4, seq_ref), (4, cot_ref), (2, taps_ref))
            for i in range(count)
        ],
        axis=1,
    )
    opened = dot_wide(jnp.concatenate([twist_ref[2], twist_ref[3]], axis=0), signals)
    cosine, sine = twist_ref[0], twist_ref[1]
    across = tables_ref[...]
    inner = jnp.concatenate([across, jnp.concatenate([-across[SIDE:], across[:SIDE]], axis=0)], axis=1)
    sends_real = lax.axis_index("chan") % 2 == 0

    def leave(filt, row, values):
        out_ref[pl.ds(THERE_ROWS * filt + row, SIDE, stride=2 * THERE_ROWS), :] = values

    for group in ((0, 1), (2, 3), (4, 5), (6, 7), (8, 9)):
        twisted = []
        for i in group:
            real = opened[:SIDE, i * SIDE : (i + 1) * SIDE]
            imag = opened[SIDE:, i * SIDE : (i + 1) * SIDE]
            twisted.append(jnp.concatenate([real * cosine + imag * sine, imag * cosine - real * sine], axis=1))
        spectra = dot_three(jnp.concatenate(twisted, axis=0), inner)
        for place, i in enumerate(group):
            real = spectra[place * SIDE : (place + 1) * SIDE, :SIDE]
            imag = spectra[place * SIDE : (place + 1) * SIDE, SIDE:]
            filt, row = place_of(i)
            if row == 8:
                leave(filt, row, jnp.where(sends_real, real, imag))
            else:
                leave(filt, row, real)
                leave(filt, row + 1, imag)


def forward_blocks(sequence, cotangent, taps):
    operands = (sequence, cotangent, taps, jnp.asarray(FORWARD_TABLES), twist_table())
    return call(forward_kernel, "forward_blocks", (OWNERS * THERE_ROWS, SIDE), operands)


def middle_kernel(in_ref, there_ref, back_ref, adjoint_ref, out_ref):
    there, back, adjoint = there_ref[...], back_ref[...], adjoint_ref[...]

    def points_of(places):
        sides = [
            jnp.concatenate(
                [
                    in_ref[pl.ds(chan * THERE_ROWS + row, BLOCKS, stride=CHAN * THERE_ROWS), :]
                    for chan, row in places(part)
                ],
                axis=1,
            )
            for part in range(2)
        ]
        points = dot_wide(there, jnp.concatenate(sides, axis=0))
        return points[:POINTS], points[POINTS:]

    def leave(table, places, real, imag):
        blocks = dot_wide(table, jnp.concatenate([real, imag], axis=0))
        for part in range(2):
            lines = slice(part * BLOCKS, (part + 1) * BLOCKS)
            for n, (chan, row) in places:
                out_ref[pl.ds(chan * BACK_ROWS + row + part, BLOCKS, stride=CHAN * BACK_ROWS), :] = blocks[
                    lines, n * SIDE : (n + 1) * SIDE
                ]

    def over_channels(values):
        return sum(values[:, n * SIDE : (n + 1) * SIDE] for n in range(len(first_kind)))

    first_kind = [(chan, row) for chan in range(CHAN) for row in (0, 2)]
    second_kind = [(chan, row + 4) for chan, row in first_kind]
    hr, hi = points_of(lambda part: [(part, 8)])
    hr, hi = (jnp.concatenate([part] * len(first_kind), axis=1) for part in (hr, hi))
    pr, pi = points_of(lambda part: [(chan, row + part) for chan, row in first_kind + second_kind])
    wide = len(first_kind) * SIDE
    xr, xi, gr, gi = pr[:, :wide], pi[:, :wide], pr[:, wide:], pi[:, wide:]
    leave(back, list(enumerate(first_kind)), hr * xr - hi * xi, hr * xi + hi * xr)
    leave(adjoint, list(enumerate(second_kind)), hr * gr + hi * gi, hr * gi - hi * gr)
    leave(
        adjoint,
        [(0, (chan, 8)) for chan in range(CHAN)],
        over_channels(xr * gr + xi * gi),
        over_channels(xr * gi - xi * gr),
    )


def middle_blocks(spectra):
    operands = (spectra,) + tuple(jnp.asarray(t) for t in BLOCK_TABLES)
    return call(middle_kernel, "middle_blocks", (OWNERS * BACK_ROWS, SIDE), operands)


def inverse_kernel(in_ref, seq_ref, cot_ref, skip_ref, inner_ref, outer_ref, twist_ref, y_ref, g_ref, f_ref):
    cosine, sine = twist_ref[0], twist_ref[1]
    inner, outer = inner_ref[...], outer_ref[...]

    columns = []
    for i in range(10):
        filt, row = place_of(i)
        both = [in_ref[pl.ds(BACK_ROWS * filt + row + p, SIDE, stride=2 * BACK_ROWS), :] for p in range(2)]
        turned = dot_three(jnp.concatenate(both, axis=1), inner)
        real, imag = turned[:, :SIDE], turned[:, SIDE:]
        column = jnp.concatenate([real * cosine - imag * sine, imag * cosine + real * sine], axis=0)
        columns.append(column)
    closed = dot_wide(outer, jnp.concatenate(columns, axis=1))

    def line(signal):
        return closed[:, signal * SIDE : (signal + 1) * SIDE].reshape(1, BLOCK)

    for c in range(4):
        gain = skip_ref[:, c : c + 1]
        y_ref[c : c + 1, :] = line(c) + gain * seq_ref[c : c + 1, :]
        g_ref[c : c + 1, :] = line(4 + c) + gain * cot_ref[c : c + 1, :]
    for c in range(2):
        f_ref[c : c + 1, :] = line(8 + c)


def inverse_blocks(spectra, sequence, cotangent, skip_gain):
    operands = (spectra, sequence, cotangent, skip_gain[None, :]) + tuple(jnp.asarray(t) for t in INVERSE_TABLES)
    return call(inverse_kernel, "inverse_blocks", ((4, BLOCK), (4, BLOCK), (2, BLOCK)), operands)


def exchange(rows, tall):
    cut = rows.reshape(OWNERS, -1, tall, SIDE)
    return lax.all_to_all(cut, ("ctx", "chan"), split_axis=0, concat_axis=0, tiled=True).reshape(rows.shape)


def body(sequence, filter_taps, skip_gain, cotangent):
    spectra = exchange(forward_blocks(sequence, cotangent, filter_taps), 1)
    products = exchange(middle_blocks(spectra), 2)
    return inverse_blocks(products, sequence, cotangent, skip_gain)


def solution(mesh):
    return jax.shard_map(
        body,
        mesh=mesh,
        in_specs=(P("chan", "ctx"), P(None, "ctx"), P("chan"), P("chan", "ctx")),
        out_specs=(P("chan", "ctx"), P("chan", "ctx"), P(None, "ctx")),
        check_vma=False,
    )
```
